128 devices in a mesh: lat: 8 (over y, core), lon: 16 (over x, z).
Axes of the slice: x: 4, y: 4, z: 4, core: 2. Of those that a mesh axis runs over, the one named last changes fastest.
Arguments:
- concentration: float32 [8, 128, 256, 128], P(None, 'lat', 'lon'), may hold values from 0.002 to 0.05
- cotangent: float32 [8, 128, 256, 128], P(None, 'lat', 'lon'), may hold values from -6 to 6
- coag_rate: float32 [8, 128, 256], P(None, 'lat', 'lon'), may hold values from 0.1 to 0.5
- weights: float32 [8, 8, 128, 256], P(None, None, 'lat', 'lon'), may hold values from 0 to 1, as said below
- departure: int32 [8, 8, 128, 256], P(None, None, 'lat', 'lon'), may hold values from 0 to 11263, as said below
- send_list: int32 [8, 16, 9, 1024], P('lat', 'lon'), may hold values from 0 to 2047
Outputs:
- adjoint_field: float32 [8, 128, 256, 128], P(None, 'lat', 'lon')
The draws below stay inside these ranges and needn't reach their ends.
Inputs may be any that keep to these rules, and one draw needn't show every extreme that they name: `departure`: an entry below 2048 names a cell of the arrival cell's own tile that differs from the arrival cell by at most one in level, in latitude row and in longitude column; an entry 2048 + b * 1024 + s names slot s of block b of the arrival cell's device. Block 4 (the device itself) is never named, nor a block whose latitude tile doesn't exist. Every device names all 1024 slots of block 5. The 8 weights of an arrival cell are trilinear weights: products of three fractions or their complements.
All inputs are finite; a program needn't handle non-finite values.
Results may differ from the reference program's by a relative error of at most 0.0003.
Values sent between devices are 32-bit elements; how exact they have to be, the bound alone decides.
A program may use at most 64 MiB of HBM per device.

```python
import math
import jax
import jax.numpy as jnp
from jax import lax

BINS = 128
LEV = 8
CORNERS = 8
BLOCKS = 9
CLAT = 16
CLON = 16
CELLS = 2048
CAP = 1024
NLAT = 128
NLON = 256
N_LAT = 8
N_LON = 16
DEVICES = 128


def corner_bits():
    corner_ids = jnp.arange(CORNERS, dtype=jnp.int32)[:, None, None, None]
    return (corner_ids // 4 % 2, corner_ids // 2 % 2, corner_ids % 2)


def draw_weights(key, part):
    fractions = jax.random.uniform(jax.random.fold_in(key, 3), (3, LEV, NLAT, NLON), jnp.float32)
    up_bit, lat_bit, lon_bit = corner_bits()
    vertical = jnp.where(up_bit == 1, fractions[0], 1.0 - fractions[0])
    meridional = jnp.where(lat_bit == 1, fractions[1], 1.0 - fractions[1])
    zonal = jnp.where(lon_bit == 1, fractions[2], 1.0 - fractions[2])
    return (vertical * meridional * zonal).astype(jnp.float32)


def live_counts(key):
    device_ids = jnp.arange(DEVICES, dtype=jnp.int32)
    lat_of = device_ids // N_LON
    block_ids = jnp.arange(BLOCKS, dtype=jnp.int32)
    src_lat = lat_of[:, None] + block_ids[None, :] // 3 - 1
    exists = (src_lat >= 0) & (src_lat < N_LAT)
    jet_band = (lat_of == N_LAT // 2) | (lat_of == N_LAT // 2 - 1)
    near_count = jax.random.randint(jax.random.fold_in(key, 1), (DEVICES, BLOCKS), CAP // 2, CAP + 1)
    counts = jnp.where(jet_band[:, None], CAP, near_count)
    counts = jnp.where(block_ids[None, :] == 5, CAP, counts)
    counts = jnp.where(exists & (block_ids[None, :] != 4), counts, 0)
    return counts.astype(jnp.int32)


def draw_departure(key, part):
    grid_shape = (CORNERS, LEV, NLAT, NLON)
    counts = live_counts(jax.random.fold_in(key, 11))
    up_bit, lat_bit, lon_bit = corner_bits()
    lev_pos = jnp.arange(LEV, dtype=jnp.int32)[None, :, None, None]
    lat_pos = jnp.arange(NLAT, dtype=jnp.int32)[None, None, :, None]
    lon_pos = jnp.arange(NLON, dtype=jnp.int32)[None, None, None, :]
    sub_keys = jax.random.split(jax.random.fold_in(key, 13), 6)
    back_lev = jax.random.randint(sub_keys[0], (1, LEV, NLAT, NLON), -1, 1)
    back_lat = jax.random.randint(sub_keys[1], (1, LEV, NLAT, NLON), -1, 1)
    back_lon = jax.random.randint(sub_keys[2], (1, LEV, NLAT, NLON), -1, 1)
    local_lev = jnp.clip(lev_pos + back_lev + up_bit, 0, LEV - 1)
    local_lat = jnp.clip(lat_pos % CLAT + back_lat + lat_bit, 0, CLAT - 1)
    local_lon = jnp.clip(lon_pos % CLON + back_lon + lon_bit, 0, CLON - 1)
    local_cell = (local_lev * CLAT + local_lat) * CLON + local_lon
    owner_dev = jnp.broadcast_to(lat_pos // CLAT * N_LON + lon_pos // CLON, grid_shape)
    block_pick = jax.random.randint(sub_keys[3], grid_shape, 0, BLOCKS)
    slot_pick = jax.random.randint(sub_keys[4], grid_shape, 0, CAP)
    coin_flip = jax.random.randint(sub_keys[5], grid_shape, 0, 2)
    is_live = slot_pick < counts[owner_dev, block_pick]
    chosen = jnp.where(is_live & (coin_flip == 1), CELLS + block_pick * CAP + slot_pick, local_cell)
    arrival = (lev_pos * CLAT + lat_pos % CLAT) * CLON + lon_pos % CLON
    forced = CELLS + 5 * CAP + arrival
    last_corner = (up_bit == 1) & (lat_bit == 1) & (lon_bit == 1)
    return jnp.where(last_corner & (arrival < CAP), forced, chosen).astype(jnp.int32)


def with_ends(array, rng, low, top_value):
    longest = array.shape.index(max(array.shape))
    spots = []
    for shift in (0, 1):
        where = [jax.random.randint(jax.random.fold_in(rng, axis), (), 0, length) for axis, length in enumerate(array.shape)]
        where[longest] = (where[longest] + shift) % array.shape[longest]
        spots.append(tuple(where))
    return array.at[spots[0]].set(low).at[spots[1]].set(top_value)


def block_scale(stream_key, shape, pieces, smallest, top_value):
    level = 1.0
    for axis_at, parts in pieces:
        draws = jax.random.uniform(jax.random.fold_in(jax.random.fold_in(stream_key, 6), axis_at), (parts,), jnp.float32, smallest / len(pieces), top_value / len(pieces))
        level = level * jnp.repeat(jnp.exp(draws), shape[axis_at] // parts).reshape((-1,) + (1,) * (len(shape) - 1 - axis_at))
    return level


def normal_values(rng, shape, spread, most, pieces=(), kind=jnp.bfloat16):
    array = jax.random.normal(rng, shape, jnp.float32) * spread
    if len(pieces) > 0:
        array = block_scale(rng, shape, pieces, -0.22, 0.18) * array
    return jnp.clip(array, min=-most, max=most).astype(kind)


def setup_inputs(seed: int = 0) -> dict:
    seeds = jax.random.split(jax.random.key(seed), 7)
    concentration = jnp.clip(jnp.exp(math.log(0.05) - 3.218876 * jax.random.uniform(seeds[0], (LEV, NLAT, NLON, BINS), jnp.float32) ** block_scale(seeds[0], (LEV, NLAT, NLON, BINS), ((1, 8), (2, 16)), -0.2, 0.2)), 0.002, 0.05)
    cotangent = normal_values(seeds[1], (LEV, NLAT, NLON, BINS), 1.0, 6.0, ((1, 8), (2, 16)), jnp.float32)
    coag_rate = jnp.clip(jnp.exp(math.log(0.5) - 1.609438 * jax.random.uniform(seeds[2], (LEV, NLAT, NLON), jnp.float32) ** block_scale(seeds[2], (LEV, NLAT, NLON), ((1, 8), (2, 16)), -0.2, 0.2)), 0.1, 0.5)
    weights = draw_weights(jax.random.fold_in(seeds[6], 71), 0)
    departure = draw_departure(jax.random.fold_in(seeds[6], 71), 0)
    send_list = with_ends(jax.random.randint(seeds[5], (N_LAT, N_LON, BLOCKS, CAP), 0, CELLS), jax.random.fold_in(seeds[5], 1), 0, CELLS - 1).astype(jnp.int32)
    return {"concentration": concentration, "cotangent": cotangent, "coag_rate": coag_rate, "weights": weights, "departure": departure, "send_list": send_list}


def coagulate(transported, coefficient):
    spectrum = jnp.fft.rfft(transported, n=2 * BINS, axis=-1)
    convolved = jnp.fft.irfft(spectrum * spectrum, n=2 * BINS, axis=-1)[:, :BINS - 1]
    gained = 0.5 * jnp.concatenate([jnp.zeros((transported.shape[0], 1), transported.dtype), convolved], axis=1)
    totals = lax.optimization_barrier(jnp.sum(transported, axis=1, keepdims=True))
    return transported + coefficient[:, None] * (gained - transported * totals)

def cell_major(field):
    trailing = field.shape[3:]
    shaped = field.reshape((LEV, N_LAT, CLAT, N_LON, CLON) + trailing)
    shaped = jnp.moveaxis(shaped, (1, 3), (0, 1))
    return shaped.reshape((N_LAT * N_LON, LEV * CLAT * CLON) + trailing)

def corner_major(field):
    shaped = field.reshape(CORNERS, LEV, N_LAT, CLAT, N_LON, CLON)
    shaped = jnp.moveaxis(shaped, (2, 4), (0, 1))
    return shaped.reshape(N_LAT * N_LON, CORNERS, LEV * CLAT * CLON)

def grid_major(field):
    shaped = field.reshape(N_LAT, N_LON, LEV, CLAT, CLON, BINS)
    shaped = jnp.moveaxis(shaped, (0, 1), (1, 3))
    return shaped.reshape(LEV, N_LAT * CLAT, N_LON * CLON, BINS)

def reference(concentration, cotangent, coag_rate, weights, departure, send_list):
    device_total = N_LAT * N_LON
    cell_total = LEV * CLAT * CLON
    device_rows = cell_major(concentration)
    device_cot = cell_major(cotangent)
    device_rate = cell_major(coag_rate)
    corner_weight = corner_major(weights)
    corner_index = corner_major(departure)
    slot_cells = send_list.reshape(device_total, BLOCKS, CAP)
    block_ids = jnp.arange(BLOCKS, dtype=jnp.int32)
    off_lat = block_ids // 3 - 1
    off_lon = block_ids % 3 - 1

    def visit(adjoint_sum, device):
        here_lat = device // N_LON
        here_lon = device % N_LON
        src_lat = here_lat + off_lat
        valid = (src_lat >= 0) & (src_lat < N_LAT)
        source = jnp.clip(src_lat, 0, N_LAT - 1) * N_LON + (here_lon + off_lon) % N_LON
        cells = slot_cells[source, block_ids]
        received = device_rows[source[:, None], cells] * valid[:, None, None].astype(jnp.float32)
        lookup_rows = jnp.concatenate([device_rows[device], received.reshape(BLOCKS * CAP, BINS)], axis=0)
        picked = lookup_rows[corner_index[device]]
        transported = lax.optimization_barrier(jnp.sum(corner_weight[device][:, :, None] * picked, axis=0))
        cell_rate = device_rate[device]
        unused_out, pullback = jax.vjp(lambda state_rows: coagulate(state_rows, cell_rate), transported)
        adjoint_rows = pullback(device_cot[device])[0]
        weighted = (corner_weight[device][:, :, None] * adjoint_rows[None]).reshape(CORNERS * cell_total, BINS)
        slot_sums = jax.ops.segment_sum(weighted, corner_index[device].reshape(-1), num_segments=cell_total + BLOCKS * CAP)
        adjoint_sum = adjoint_sum.at[device].add(slot_sums[:cell_total])
        block_sums = slot_sums[cell_total:].reshape(BLOCKS, CAP, BINS) * valid[:, None, None].astype(jnp.float32)
        adjoint_sum = adjoint_sum.at[source[:, None], cells].add(block_sums)
        return (adjoint_sum, None)
    adjoint_sum, unused_tail = lax.scan(visit, jnp.zeros((device_total, cell_total, BINS), jnp.float32), jnp.arange(device_total, dtype=jnp.int32))
    return grid_major(adjoint_sum)
```

```python
import functools

import jax
import jax.numpy as jnp
import numpy as np
from jax import lax
from jax.experimental import pallas as pl
from jax.experimental.pallas import tpu as pltpu
from jax.sharding import PartitionSpec as P

MESH = pl.DeviceIdType.MESH
F32 = jnp.float32
BF16 = jnp.bfloat16
I16 = jnp.int16
I32 = jnp.int32
SMEM = pl.BlockSpec(memory_space=pltpu.SMEM)
VMEM = pl.BlockSpec(memory_space=pltpu.VMEM)
ANY = pl.BlockSpec(memory_space=pl.ANY)
ORDER = ((0, 0), (2, 2), (0, 2), (2, 0), (1, 0), (1, 2), (0, 1), (2, 1))
ACCS = 4


def split(x):
    hi = x.astype(BF16)
    return hi, (x - hi.astype(F32)).astype(BF16)


def spectral_tables(bins):
    period = 2 * bins
    k = np.arange(bins)
    n = np.arange(bins)[:, None]
    angle = 2.0 * np.pi * (n * k % period) / period
    sine = -np.sin(angle)
    sine[:, 0] = np.cos(np.pi * np.arange(bins))
    forward = np.concatenate([np.cos(angle), sine], axis=1)
    lag = np.arange(1, bins + 1)[None, :]
    back = 2.0 * np.pi * (k[:, None] * lag % period) / period
    scale = np.where(k == 0, 1.0, 2.0)[:, None] / period
    real = np.cos(back) * scale
    imag = -np.sin(back) * scale
    imag[0] = np.cos(np.pi * lag[0]) / period
    inverse = np.concatenate([real, imag], axis=0)
    return forward.astype(np.float32), inverse.astype(np.float32)


class Place:
    def __init__(self, n_lat, n_lon):
        self.lat = lax.axis_index("lat")
        self.lon = lax.axis_index("lon")
        self.n_lat = n_lat
        self.n_lon = n_lon

    def has(self, u):
        there = self.lat + u - 1
        return (there >= 0) & (there < self.n_lat)

    def at(self, u, v):
        return (self.lat + u - 1, lax.rem(self.lon + v - 1 + self.n_lon, self.n_lon))

    def greet(self):
        barrier = pltpu.get_barrier_semaphore()
        for u, v in ORDER:
            @pl.when(self.has(u))
            def _():
                pl.semaphore_signal(barrier, inc=1, device_id=self.at(u, v), device_id_type=MESH)
        count = jnp.where(self.lat > 0, 3, 0) + jnp.where(self.lat < self.n_lat - 1, 3, 0) + 2
        pl.semaphore_wait(barrier, count)


def send_kernel(n_lat, n_lon, cells, cap, slots, own, table, rows, own_sem, send_sem, recv_sem):
    place = Place(n_lat, n_lon)
    place.greet()
    keep = pltpu.make_async_copy(own, table.at[pl.ds(0, cells)], own_sem)
    keep.start()

    def copy(u, v):
        b = 3 * u + v
        return pltpu.make_async_remote_copy(
            src_ref=rows.at[b], dst_ref=table.at[pl.ds(cells + b * cap, cap)], send_sem=send_sem.at[b],
            recv_sem=recv_sem.at[b], device_id=place.at(2 - u, 2 - v), device_id_type=MESH)

    for u, v in ORDER:
        @pl.when(place.has(2 - u))
        def _():
            b = 3 * u + v
            step = 32

            def gather(i, carry):
                for j in range(step):
                    s = i * step + j
                    rows[b, pl.ds(s, 1), :] = own[pl.ds(slots[b * cap + s], 1), :]
                return carry

            lax.fori_loop(0, cap // step, gather, 0)
            copy(u, v).start()
    keep.wait()
    for u, v in ORDER:
        @pl.when(place.has(u))
        def _():
            copy(u, v).wait_recv()

        @pl.when(place.has(2 - u))
        def _():
            copy(u, v).wait_send()


def cell_kernel(cells, corners, index, weight, table, cot, rate, fwd_hi, fwd_lo, inv_hi, inv_lo, out, state, *more):
    accs = (out,) + more
    step = 4

    def gather(i, carry):
        for j in range(step):
            a = i * step + j
            total = None
            for k in range(corners):
                row = table[pl.ds(index[k * cells + a], 1), :] * weight[k * cells + a]
                total = row if total is None else total + row
            state[pl.ds(a, 1), :] = total
        return carry

    lax.fori_loop(0, cells // step, gather, 0)
    tile = 256
    bins = cot.shape[1]
    first = lax.broadcasted_iota(I32, (tile, bins), 1) == 0

    def dot3(x, hi, lo):
        xh, xl = split(x)
        out = jnp.dot(xh, hi[...], preferred_element_type=F32)
        out += jnp.dot(xl, hi[...], preferred_element_type=F32)
        return out + jnp.dot(xh, lo[...], preferred_element_type=F32)

    def react(i, carry):
        here = pl.ds(pl.multiple_of(i * tile, tile), tile)
        t = state[here, :]
        c = cot[here, :]
        ts = dot3(t, fwd_hi, fwd_lo)
        cs = dot3(c, fwd_hi, fwd_lo)
        ta, tb, ca, cb = ts[:, :bins], ts[:, bins:], cs[:, :bins], cs[:, bins:]
        both = tb * cb
        real = ta * ca + jnp.where(first, 0.0, both)
        imag = jnp.where(first, both, ta * cb - tb * ca)
        lagged = dot3(jnp.concatenate([real, imag], axis=1), inv_hi, inv_lo)
        totals = jnp.sum(t, axis=1, keepdims=True)
        weighed = jnp.sum(t * c, axis=1, keepdims=True)
        state[here, :] = c + rate[here, :] * (lagged - totals * c - weighed)
        return carry

    lax.fori_loop(0, cells // tile, react, 0)
    chunk = 512
    for acc in accs:
        def clear(i, carry):
            acc[pl.ds(pl.multiple_of(i * chunk, chunk), chunk), :] = jnp.zeros((chunk, bins), F32)
            return carry

        lax.fori_loop(0, out.shape[0] // chunk, clear, 0)
    step = 2

    def scatter(i, carry):
        for j in range(step):
            a = i * step + j
            row = state[pl.ds(a, 1), :]
            for k in range(0, corners, ACCS):
                at = [pl.ds(index[(k + m) * cells + a], 1) for m in range(ACCS)]
                new = [accs[m][at[m], :] + row * weight[(k + m) * cells + a] for m in range(ACCS)]
                for m in range(ACCS):
                    accs[m][at[m], :] = new[m]
        return carry

    lax.fori_loop(0, cells // step, scatter, 0)

    def merge(i, carry):
        here = pl.ds(pl.multiple_of(i * chunk, chunk), chunk)
        total = out[here, :]
        for acc in more:
            total = total + acc[here, :]
        out[here, :] = total
        return carry

    lax.fori_loop(0, out.shape[0] // chunk, merge, 0)


def return_kernel(n_lat, n_lon, cells, cap, slots, sums, out, back, send_sem, recv_sem):
    place = Place(n_lat, n_lon)
    place.greet()

    def copy(u, v):
        b = 3 * u + v
        return pltpu.make_async_remote_copy(
            src_ref=sums.at[pl.ds(cells + b * cap, cap)], dst_ref=back.at[b], send_sem=send_sem.at[b],
            recv_sem=recv_sem.at[b], device_id=place.at(u, v), device_id_type=MESH)

    for u, v in ORDER:
        @pl.when(place.has(u))
        def _():
            copy(u, v).start()
    out[...] = sums[pl.ds(0, cells), :]
    tile = 256
    bins = out.shape[1]
    number = lax.broadcasted_iota(I32, (tile, cap), 0).astype(I16)
    for u, v in ORDER[6:] + ORDER[:6]:
        @pl.when(place.has(2 - u))
        def _():
            b = 3 * u + v
            copy(u, v).wait_recv()
            rows = jnp.concatenate(split(back[b]), axis=1)
            named = slots[pl.ds(b, 1), :]

            def add(i, carry):
                here = pl.ds(pl.multiple_of(i * tile, tile), tile)
                hit = (named - i * tile).astype(I16) == number
                pick = jnp.where(hit, jnp.ones((), BF16), jnp.zeros((), BF16))
                got = jnp.dot(pick, rows, preferred_element_type=F32)
                out[here, :] += got[:, :bins] + got[:, bins:]
                return carry

            lax.fori_loop(0, cells // tile, add, 0)
    for u, v in ORDER:
        @pl.when(place.has(u))
        def _():
            copy(u, v).wait_send()


def on_device(n_lat, n_lon, concentration, cotangent, coag_rate, weights, departure, send_list):
    levels, lat_cells, lon_cells, bins = concentration.shape
    cells = levels * lat_cells * lon_cells
    blocks, cap = send_list.shape[2:]
    corners = departure.shape[0]
    entries = cells + blocks * cap
    own = concentration.reshape(cells, bins)
    dma = pltpu.SemaphoreType.DMA
    table = pl.pallas_call(
        functools.partial(send_kernel, n_lat, n_lon, cells, cap),
        out_shape=jax.ShapeDtypeStruct((entries, bins), F32),
        in_specs=[SMEM, VMEM], out_specs=ANY,
        scratch_shapes=[pltpu.VMEM((blocks, cap, bins), F32), dma, dma((blocks,)), dma((blocks,))],
        compiler_params=pltpu.CompilerParams(
            collective_id=0, has_side_effects=True, vmem_limit_bytes=16 * 2**20),
    )(send_list.reshape(blocks * cap), own)
    forward, inverse = spectral_tables(bins)
    fwd_hi, fwd_lo = split(jnp.asarray(forward))
    inv_hi, inv_lo = split(jnp.asarray(inverse))
    sums = pl.pallas_call(
        functools.partial(cell_kernel, cells, corners),
        out_shape=jax.ShapeDtypeStruct((entries, bins), F32),
        in_specs=[SMEM, SMEM] + [VMEM] * 7, out_specs=VMEM,
        scratch_shapes=[pltpu.VMEM((cells, bins), F32)] + [pltpu.VMEM((entries, bins), F32)] * (ACCS - 1),
        compiler_params=pltpu.CompilerParams(vmem_limit_bytes=48 * 2**20),
    )(departure.reshape(-1), weights.reshape(-1), table, cotangent.reshape(cells, bins),
      coag_rate.reshape(cells, 1), fwd_hi, fwd_lo, inv_hi, inv_lo)
    total = pl.pallas_call(
        functools.partial(return_kernel, n_lat, n_lon, cells, cap),
        out_shape=jax.ShapeDtypeStruct((cells, bins), F32),
        in_specs=[VMEM, VMEM], out_specs=VMEM,
        scratch_shapes=[pltpu.VMEM((blocks, cap, bins), F32), dma((blocks,)), dma((blocks,))],
        compiler_params=pltpu.CompilerParams(
            collective_id=1, has_side_effects=True, vmem_limit_bytes=32 * 2**20),
    )(send_list.reshape(blocks, cap), sums)
    return total.reshape(levels, lat_cells, lon_cells, bins)


def solution(mesh):
    grid = P(None, "lat", "lon", None)
    field = P(None, "lat", "lon")
    corner = P(None, None, "lat", "lon")
    lists = P("lat", "lon", None, None)
    body = functools.partial(on_device, mesh.shape["lat"], mesh.shape["lon"])
    return jax.shard_map(
        body, mesh=mesh, in_specs=(grid, grid, field, corner, corner, lists), out_specs=grid, check_vma=False)
```

```python
import functools

import jax
import jax.numpy as jnp
import numpy as np
from jax import lax
from jax.experimental import pallas as pl
from jax.experimental.pallas import tpu as pltpu
from jax.sharding import PartitionSpec as P

MESH = pl.DeviceIdType.MESH
F32 = jnp.float32
BF16 = jnp.bfloat16
I16 = jnp.int16
I32 = jnp.int32
SMEM = pl.BlockSpec(memory_space=pltpu.SMEM)
VMEM = pl.BlockSpec(memory_space=pltpu.VMEM)
ANY = pl.BlockSpec(memory_space=pl.ANY)
ORDER = ((0, 0), (2, 2), (0, 2), (2, 0), (1, 0), (1, 2), (0, 1), (2, 1))
ROW_BITS = 14
ROW_MASK = 2**ROW_BITS - 1
WORD_UNIT = 2.0**-31


def split(x):
    hi = x.astype(BF16)
    return hi, (x - hi.astype(F32)).astype(BF16)


def spectral_tables(bins):
    period = 2 * bins
    k = np.arange(bins)
    n = np.arange(bins)[:, None]
    angle = 2.0 * np.pi * (n * k % period) / period
    sine = -np.sin(angle)
    sine[:, 0] = np.cos(np.pi * np.arange(bins))
    forward = np.concatenate([np.cos(angle), sine], axis=1)
    lag = np.arange(1, bins + 1)[None, :]
    back = 2.0 * np.pi * (k[:, None] * lag % period) / period
    scale = np.where(k == 0, 1.0, 2.0)[:, None] / period
    real = np.cos(back) * scale
    imag = -np.sin(back) * scale
    imag[0] = np.cos(np.pi * lag[0]) / period
    inverse = np.concatenate([real, imag], axis=0)
    return forward.astype(np.float32), inverse.astype(np.float32)


def slot(u, v):
    b = 3 * u + v
    return b - (b > 4)


class Place:
    def __init__(self, n_lat, n_lon):
        self.lat = lax.axis_index("lat")
        self.lon = lax.axis_index("lon")
        self.n_lat = n_lat
        self.n_lon = n_lon

    def has(self, u):
        there = self.lat + u - 1
        return (there >= 0) & (there < self.n_lat)

    def at(self, u, v):
        return (self.lat + u - 1, lax.rem(self.lon + v - 1 + self.n_lon, self.n_lon))

    def greet(self):
        barrier = pltpu.get_barrier_semaphore()
        for u, v in ORDER:
            @pl.when(self.has(u))
            def _():
                pl.semaphore_signal(barrier, inc=1, device_id=self.at(u, v), device_id_type=MESH)
        count = jnp.where(self.lat > 0, 3, 0) + jnp.where(self.lat < self.n_lat - 1, 3, 0) + 2
        pl.semaphore_wait(barrier, count)


def send_kernel(n_lat, n_lon, cells, cap, slots, own, table, rows, own_sem, send_sem, recv_sem):
    place = Place(n_lat, n_lon)
    place.greet()
    keep = pltpu.make_async_copy(own, table.at[pl.ds(0, cells)], own_sem)
    keep.start()

    def copy(u, v):
        b = 3 * u + v
        return pltpu.make_async_remote_copy(
            src_ref=rows.at[b], dst_ref=table.at[pl.ds(cells + slot(u, v) * cap, cap)], send_sem=send_sem.at[b],
            recv_sem=recv_sem.at[b], device_id=place.at(2 - u, 2 - v), device_id_type=MESH)

    for u, v in ORDER:
        @pl.when(place.has(2 - u))
        def _():
            b = 3 * u + v
            step = 32

            def gather(i, carry):
                for j in range(step):
                    s = i * step + j
                    rows[b, pl.ds(s, 1), :] = own[pl.ds(slots[b * cap + s], 1), :]
                return carry

            lax.fori_loop(0, cap // step, gather, 0)
            copy(u, v).start()
    keep.wait()
    for u, v in ORDER:
        @pl.when(place.has(u))
        def _():
            copy(u, v).wait_recv()

        @pl.when(place.has(2 - u))
        def _():
            copy(u, v).wait_send()


def cell_kernel(cells, corners, *refs):
    (words, table_hbm, cot, rate, fwd_hi, fwd_lo, inv_hi, inv_lo, sums), refs = refs[:9], refs[9:]
    table, state, refs = refs[0], refs[1], refs[2:]
    accs, refs = refs[:corners], refs[corners:]
    word, (word_sem, table_sem, out_sem) = refs[:corners], refs[corners:]
    entries, bins = table.shape
    load = pltpu.make_async_copy(table_hbm, table, table_sem)
    load.start()
    loads = [pltpu.make_async_copy(words.at[pl.ds(k * cells, cells)], word[k], word_sem.at[k]) for k in range(corners)]
    for copy in loads:
        copy.start()
    chunk = 512

    def clear(i, carry):
        for acc in accs:
            acc[pl.ds(pl.multiple_of(i * chunk, chunk), chunk), :] = jnp.zeros((chunk, bins), F32)
        return carry

    lax.fori_loop(0, entries // chunk, clear, 0)
    for copy in loads:
        copy.wait()
    load.wait()
    step = 4

    def gather(i, carry):
        for j in range(step):
            a = i * step + j
            total = None
            for k in range(corners):
                code = word[k][a]
                row = table[pl.ds(code & ROW_MASK, 1), :] * jnp.full((1, bins), code, I32).astype(F32)
                total = row if total is None else total + row
            state[pl.ds(a, 1), :] = total
        return carry

    lax.fori_loop(0, cells // step, gather, 0)
    tile = 256
    first = lax.broadcasted_iota(I32, (tile, bins), 1) == 0

    def dot3(x, hi, lo):
        xh, xl = split(x)
        out = jnp.dot(xh, hi[...], preferred_element_type=F32)
        out += jnp.dot(xl, hi[...], preferred_element_type=F32)
        return out + jnp.dot(xh, lo[...], preferred_element_type=F32)

    def react(i, carry):
        here = pl.ds(pl.multiple_of(i * tile, tile), tile)
        t = state[here, :] * WORD_UNIT
        c = cot[here, :]
        ts = dot3(t, fwd_hi, fwd_lo)
        cs = dot3(c, fwd_hi, fwd_lo)
        ta, tb, ca, cb = ts[:, :bins], ts[:, bins:], cs[:, :bins], cs[:, bins:]
        both = tb * cb
        real = ta * ca + jnp.where(first, 0.0, both)
        imag = jnp.where(first, both, ta * cb - tb * ca)
        lagged = dot3(jnp.concatenate([real, imag], axis=1), inv_hi, inv_lo)
        totals = jnp.sum(t, axis=1, keepdims=True)
        weighed = jnp.sum(t * c, axis=1, keepdims=True)
        state[here, :] = (c + rate[here, :] * (lagged - totals * c - weighed)) * WORD_UNIT
        return carry

    lax.fori_loop(0, cells // tile, react, 0)
    step = 4

    def scatter(i, carry):
        for j in range(step):
            a = i * step + j
            row = state[pl.ds(a, 1), :]
            codes = [word[k][a] for k in range(corners)]
            at = [pl.ds(code & ROW_MASK, 1) for code in codes]
            new = [accs[k][at[k], :] + row * jnp.full((1, bins), codes[k], I32).astype(F32) for k in range(corners)]
            for k in range(corners):
                accs[k][at[k], :] = new[k]
        return carry

    lax.fori_loop(0, cells // step, scatter, 0)

    def merge(i, carry):
        here = pl.ds(pl.multiple_of(i * chunk, chunk), chunk)
        total = accs[0][here, :]
        for acc in accs[1:]:
            total = total + acc[here, :]
        table[here, :] = total
        pltpu.make_async_copy(table.at[here], sums.at[here], out_sem).start()
        return carry

    lax.fori_loop(0, entries // chunk, merge, 0)
    pltpu.make_async_copy(table, sums, out_sem).wait()


def return_kernel(n_lat, n_lon, cells, cap, slots, sums, out, back, own_sem, send_sem, recv_sem):
    place = Place(n_lat, n_lon)
    place.greet()

    def copy(u, v):
        b = 3 * u + v
        return pltpu.make_async_remote_copy(
            src_ref=sums.at[pl.ds(cells + slot(u, v) * cap, cap)], dst_ref=back.at[b], send_sem=send_sem.at[b],
            recv_sem=recv_sem.at[b], device_id=place.at(u, v), device_id_type=MESH)

    for u, v in ORDER:
        @pl.when(place.has(u))
        def _():
            copy(u, v).start()
    keep = pltpu.make_async_copy(sums.at[pl.ds(0, cells)], out, own_sem)
    keep.start()
    keep.wait()
    tile = 256
    bins = out.shape[1]
    number = lax.broadcasted_iota(I32, (tile, cap), 0).astype(I16)
    for u, v in ORDER[6:] + ORDER[:6]:
        @pl.when(place.has(2 - u))
        def _():
            b = 3 * u + v
            copy(u, v).wait_recv()
            rows = jnp.concatenate(split(back[b]), axis=1)
            named = slots[pl.ds(b, 1), :]

            def add(i, carry):
                here = pl.ds(pl.multiple_of(i * tile, tile), tile)
                hit = (named - i * tile).astype(I16) == number
                pick = jnp.where(hit, jnp.ones((), BF16), jnp.zeros((), BF16))
                got = jnp.dot(pick, rows, preferred_element_type=F32)
                out[here, :] += got[:, :bins] + got[:, bins:]
                return carry

            lax.fori_loop(0, cells // tile, add, 0)
    for u, v in ORDER:
        @pl.when(place.has(u))
        def _():
            copy(u, v).wait_send()


def on_device(n_lat, n_lon, concentration, cotangent, coag_rate, weights, departure, send_list):
    levels, lat_cells, lon_cells, bins = concentration.shape
    cells = levels * lat_cells * lon_cells
    blocks, cap = send_list.shape[2:]
    corners = departure.shape[0]
    entries = cells + (blocks - 1) * cap
    own = concentration.reshape(cells, bins)
    dma = pltpu.SemaphoreType.DMA
    table = pl.pallas_call(
        functools.partial(send_kernel, n_lat, n_lon, cells, cap),
        out_shape=jax.ShapeDtypeStruct((entries, bins), F32),
        in_specs=[SMEM, VMEM], out_specs=ANY,
        scratch_shapes=[pltpu.VMEM((blocks, cap, bins), F32), dma, dma((blocks,)), dma((blocks,))],
        compiler_params=pltpu.CompilerParams(
            collective_id=0, has_side_effects=True, vmem_limit_bytes=56 * 2**20),
    )(send_list.reshape(blocks * cap), own)
    forward, inverse = spectral_tables(bins)
    fwd_hi, fwd_lo = split(jnp.asarray(forward))
    inv_hi, inv_lo = split(jnp.asarray(inverse))
    row = jnp.where(departure < cells + 5 * cap, departure, departure - cap)
    high = jnp.round((weights * 2.0**31 - row.astype(F32)) * 2.0**-ROW_BITS)
    high = jnp.clip(high, 0.0, 2.0 ** (31 - ROW_BITS) - 1.0).astype(I32)
    words = (high * 2**ROW_BITS + row).reshape(-1)
    sums = pl.pallas_call(
        functools.partial(cell_kernel, cells, corners),
        out_shape=jax.ShapeDtypeStruct((entries, bins), F32),
        in_specs=[ANY, ANY] + [VMEM] * 6, out_specs=ANY,
        scratch_shapes=[pltpu.VMEM((entries, bins), F32), pltpu.VMEM((cells, bins), F32)]
        + [pltpu.VMEM((entries, bins), F32)] * corners + [pltpu.SMEM((cells,), I32)] * corners
        + [dma((corners,)), dma, dma],
        compiler_params=pltpu.CompilerParams(vmem_limit_bytes=56 * 2**20),
    )(words, table, cotangent.reshape(cells, bins), coag_rate.reshape(cells, 1), fwd_hi, fwd_lo, inv_hi, inv_lo)
    total = pl.pallas_call(
        functools.partial(return_kernel, n_lat, n_lon, cells, cap),
        out_shape=jax.ShapeDtypeStruct((cells, bins), F32),
        in_specs=[VMEM, ANY], out_specs=VMEM,
        scratch_shapes=[pltpu.VMEM((blocks, cap, bins), F32), dma, dma((blocks,)), dma((blocks,))],
        compiler_params=pltpu.CompilerParams(
            collective_id=1, has_side_effects=True, vmem_limit_bytes=56 * 2**20),
    )(send_list.reshape(blocks, cap), sums)
    return total.reshape(levels, lat_cells, lon_cells, bins)


def solution(mesh):
    grid = P(None, "lat", "lon", None)
    field = P(None, "lat", "lon")
    corner = P(None, None, "lat", "lon")
    lists = P("lat", "lon", None, None)
    body = functools.partial(on_device, mesh.shape["lat"], mesh.shape["lon"])
    return jax.shard_map(
        body, mesh=mesh, in_specs=(grid, grid, field, corner, corner, lists), out_specs=grid, check_vma=False)
```

```python
import functools

import jax
import jax.numpy as jnp
import numpy as np
from jax import lax
from jax.experimental import pallas as pl
from jax.experimental.pallas import tpu as pltpu
from jax.sharding import PartitionSpec as P

MESH = pl.DeviceIdType.MESH
F32 = jnp.float32
BF16 = jnp.bfloat16
I16 = jnp.int16
I32 = jnp.int32
SMEM = pl.BlockSpec(memory_space=pltpu.SMEM)
VMEM = pl.BlockSpec(memory_space=pltpu.VMEM)
ANY = pl.BlockSpec(memory_space=pl.ANY)
ORDER = ((0, 0), (2, 2), (0, 2), (2, 0), (1, 0), (1, 2), (0, 1), (2, 1))


def split(x):
    hi = x.astype(BF16)
    return hi, (x - hi.astype(F32)).astype(BF16)


def spectral_tables(bins):
    period = 2 * bins
    k = np.arange(bins)
    n = np.arange(bins)[:, None]
    angle = 2.0 * np.pi * (n * k % period) / period
    sine = -np.sin(angle)
    sine[:, 0] = np.cos(np.pi * np.arange(bins))
    forward = np.concatenate([np.cos(angle), sine], axis=1)
    lag = np.arange(1, bins + 1)[None, :]
    back = 2.0 * np.pi * (k[:, None] * lag % period) / period
    scale = np.where(k == 0, 1.0, 2.0)[:, None] / period
    real = np.cos(back) * scale
    imag = -np.sin(back) * scale
    imag[0] = np.cos(np.pi * lag[0]) / period
    inverse = np.concatenate([real, imag], axis=0)
    return forward.astype(np.float32), inverse.astype(np.float32)


def slot(u, v):
    b = 3 * u + v
    return b - (b > 4)


class Place:
    def __init__(self, n_lat, n_lon):
        self.lat = lax.axis_index("lat")
        self.lon = lax.axis_index("lon")
        self.n_lat = n_lat
        self.n_lon = n_lon

    def has(self, u):
        there = self.lat + u - 1
        return (there >= 0) & (there < self.n_lat)

    def at(self, u, v):
        return (self.lat + u - 1, lax.rem(self.lon + v - 1 + self.n_lon, self.n_lon))

    def greet(self):
        barrier = pltpu.get_barrier_semaphore()
        for u, v in ORDER:
            @pl.when(self.has(u))
            def _():
                pl.semaphore_signal(barrier, inc=1, device_id=self.at(u, v), device_id_type=MESH)
        count = jnp.where(self.lat > 0, 3, 0) + jnp.where(self.lat < self.n_lat - 1, 3, 0) + 2
        pl.semaphore_wait(barrier, count)


def send_kernel(n_lat, n_lon, cells, cap, slots, own, weights, table, spread, rows, wide, own_sem, wide_sem, send_sem,
                recv_sem):
    place = Place(n_lat, n_lon)
    place.greet()
    keep = pltpu.make_async_copy(own, table.at[pl.ds(0, cells)], own_sem)
    keep.start()

    def copy(u, v):
        b = 3 * u + v
        return pltpu.make_async_remote_copy(
            src_ref=rows.at[b], dst_ref=table.at[pl.ds(cells + slot(u, v) * cap, cap)], send_sem=send_sem.at[b],
            recv_sem=recv_sem.at[b], device_id=place.at(2 - u, 2 - v), device_id_type=MESH)

    for u, v in ORDER:
        @pl.when(place.has(2 - u))
        def _():
            b = 3 * u + v
            step = 32

            def gather(i, carry):
                for j in range(step):
                    s = i * step + j
                    rows[b, pl.ds(s, 1), :] = own[pl.ds(slots[b * cap + s], 1), :]
                return carry

            lax.fori_loop(0, cap // step, gather, 0)
            copy(u, v).start()
    corners, levels, high, long = weights.shape
    bins = own.shape[1]
    per_level = high * long * corners

    def widen(level, carry):
        values = weights[:, level]
        start = level * per_level
        for i in range(high):
            line = values[:, i, :]
            for j in range(long):
                at = pl.multiple_of(start + (i * long + j) * corners, corners)
                wide[pl.ds(at, corners), :] = jnp.broadcast_to(line[:, j:j + 1], (corners, bins))
        return carry

    lax.fori_loop(0, levels, widen, 0)
    store = pltpu.make_async_copy(wide, spread, wide_sem)
    store.start()
    keep.wait()
    store.wait()
    for u, v in ORDER:
        @pl.when(place.has(u))
        def _():
            copy(u, v).wait_recv()

        @pl.when(place.has(2 - u))
        def _():
            copy(u, v).wait_send()


def cell_kernel(cells, corners, *refs):
    (named, spread, table_hbm, cot, rate, fwd_hi, fwd_lo, inv_hi, inv_lo, sums), refs = refs[:10], refs[10:]
    (table, state, wide), refs = refs[:3], refs[3:]
    accs, refs = refs[:corners], refs[corners:]
    index, (index_sem, table_sem, wide_sem, out_sem) = refs[:corners], refs[corners:]
    entries, bins = table.shape
    load = pltpu.make_async_copy(table_hbm, table, table_sem)
    load.start()
    loads = [pltpu.make_async_copy(named.at[pl.ds(k * cells, cells)], index[k], index_sem.at[k]) for k in range(corners)]
    for copy in loads:
        copy.start()
    parts = 4
    part = cells // parts
    wides = []
    for p in range(parts):
        here = pl.ds(p * part * corners, part * corners)
        wides.append(pltpu.make_async_copy(spread.at[here], wide.at[here], wide_sem.at[p]))
        wides[p].start()
    for copy in loads:
        copy.wait()
    load.wait()
    step = 16
    clear = entries * step // cells

    def gather(i, carry):
        for j in range(step):
            a = i * step + j
            total = None
            for k in range(corners):
                row = table[pl.ds(index[k][a], 1), :] * wide[pl.ds(a * corners + k, 1), :]
                total = row if total is None else total + row
            state[pl.ds(a, 1), :] = total
        for acc in accs:
            acc[pl.ds(pl.multiple_of(i * clear, clear), clear), :] = jnp.zeros((clear, bins), F32)
        return carry

    for p in range(parts):
        wides[p].wait()
        lax.fori_loop(p * part // step, (p + 1) * part // step, gather, 0)
    tile = 256
    first = lax.broadcasted_iota(I32, (tile, bins), 1) == 0
    diagonal = lax.broadcasted_iota(I32, (bins, bins), 0) == lax.broadcasted_iota(I32, (bins, bins), 1)

    def dot3(x, hi, lo):
        xh, xl = split(x)
        out = jnp.dot(xh, hi[...], preferred_element_type=F32)
        out += jnp.dot(xl, hi[...], preferred_element_type=F32)
        return out + jnp.dot(xh, lo[...], preferred_element_type=F32)

    def react(i, carry):
        here = pl.ds(pl.multiple_of(i * tile, tile), tile)
        t = state[here, :]
        c = cot[here, :]
        ts = dot3(t, fwd_hi, fwd_lo)
        cs = dot3(c, fwd_hi, fwd_lo)
        ta, tb, ca, cb = ts[:, :bins], ts[:, bins:], cs[:, :bins], cs[:, bins:]
        both = tb * cb
        real = ta * ca + jnp.where(first, 0.0, both)
        imag = jnp.where(first, both, ta * cb - tb * ca)
        lagged = dot3(jnp.concatenate([real, imag], axis=1), inv_hi, inv_lo)
        totals = jnp.sum(t, axis=1, keepdims=True)
        weighed = jnp.sum(t * c, axis=1, keepdims=True)
        speed = [jnp.sum(jnp.where(diagonal, rate[pl.ds(i * (tile // bins) + h, 1), :], 0.0), axis=1, keepdims=True)
                 for h in range(tile // bins)]
        state[here, :] = c + jnp.concatenate(speed, axis=0) * (lagged - totals * c - weighed)
        return carry

    lax.fori_loop(0, cells // tile, react, 0)

    def scatter(i, carry):
        for j in range(step):
            a = i * step + j
            row = state[pl.ds(a, 1), :]
            at = [pl.ds(index[k][a], 1) for k in range(corners)]
            new = [accs[k][at[k], :] + row * wide[pl.ds(a * corners + k, 1), :] for k in range(corners)]
            for k in range(corners):
                accs[k][at[k], :] = new[k]
        return carry

    lax.fori_loop(0, cells // step, scatter, 0)
    chunk = 512

    def merge(i, carry):
        here = pl.ds(pl.multiple_of(i * chunk, chunk), chunk)
        total = accs[0][here, :]
        for acc in accs[1:]:
            total = total + acc[here, :]
        table[here, :] = total
        pltpu.make_async_copy(table.at[here], sums.at[here], out_sem).start()
        return carry

    lax.fori_loop(0, entries // chunk, merge, 0)
    pltpu.make_async_copy(table, sums, out_sem).wait()


def return_kernel(n_lat, n_lon, cells, cap, slots, sums, out, back, send_sem, recv_sem):
    place = Place(n_lat, n_lon)
    place.greet()

    def copy(u, v):
        b = 3 * u + v
        return pltpu.make_async_remote_copy(
            src_ref=sums.at[pl.ds(cells + slot(u, v) * cap, cap)], dst_ref=back.at[b], send_sem=send_sem.at[b],
            recv_sem=recv_sem.at[b], device_id=place.at(u, v), device_id_type=MESH)

    for u, v in ORDER:
        @pl.when(place.has(u))
        def _():
            copy(u, v).start()
    out[...] = jnp.zeros_like(out)
    tile = 256
    bins = out.shape[1]
    number = lax.broadcasted_iota(I32, (tile, bins), 0).astype(I16)
    for u, v in ORDER[6:] + ORDER[:6]:
        @pl.when(place.has(2 - u))
        def _():
            b = 3 * u + v
            copy(u, v).wait_recv()
            rows = jnp.concatenate(split(back[b]), axis=1)
            lines = cap // bins
            named = [slots[pl.ds(b * lines + q, 1), :] for q in range(lines)]

            def add(i, carry):
                here = pl.ds(pl.multiple_of(i * tile, tile), tile)
                hits = [(line - i * tile).astype(I16) == number for line in named]
                pick = jnp.concatenate(
                    [jnp.where(hit, jnp.ones((), BF16), jnp.zeros((), BF16)) for hit in hits], axis=1)
                got = jnp.dot(pick, rows, preferred_element_type=F32)
                out[here, :] += got[:, :bins] + got[:, bins:]
                return carry

            lax.fori_loop(0, cells // tile, add, 0)
    for u, v in ORDER:
        @pl.when(place.has(u))
        def _():
            copy(u, v).wait_send()


def on_device(n_lat, n_lon, concentration, cotangent, coag_rate, weights, departure, send_list):
    levels, lat_cells, lon_cells, bins = concentration.shape
    cells = levels * lat_cells * lon_cells
    blocks, cap = send_list.shape[2:]
    corners = departure.shape[0]
    entries = cells + (blocks - 1) * cap
    own = concentration.reshape(cells, bins)
    dma = pltpu.SemaphoreType.DMA
    table, spread = pl.pallas_call(
        functools.partial(send_kernel, n_lat, n_lon, cells, cap),
        out_shape=[jax.ShapeDtypeStruct((entries, bins), F32), jax.ShapeDtypeStruct((cells * corners, bins), F32)],
        in_specs=[SMEM, VMEM, VMEM], out_specs=[ANY, ANY],
        scratch_shapes=[pltpu.VMEM((blocks, cap, bins), F32), pltpu.VMEM((cells * corners, bins), F32), dma, dma,
                        dma((blocks,)), dma((blocks,))],
        compiler_params=pltpu.CompilerParams(
            collective_id=0, has_side_effects=True, vmem_limit_bytes=56 * 2**20),
    )(send_list.reshape(blocks * cap), own, weights)
    forward, inverse = spectral_tables(bins)
    fwd_hi, fwd_lo = split(jnp.asarray(forward))
    inv_hi, inv_lo = split(jnp.asarray(inverse))
    named = jnp.where(departure < cells + 5 * cap, departure, departure - cap).reshape(-1)
    sums = pl.pallas_call(
        functools.partial(cell_kernel, cells, corners),
        out_shape=jax.ShapeDtypeStruct((entries, bins), F32),
        in_specs=[ANY, ANY, ANY] + [VMEM] * 6, out_specs=ANY,
        scratch_shapes=[pltpu.VMEM((entries, bins), F32), pltpu.VMEM((cells, bins), F32),
                        pltpu.VMEM((cells * corners, bins), F32)]
        + [pltpu.VMEM((entries, bins), F32)] * corners + [pltpu.SMEM((cells,), I32)] * corners
        + [dma((corners,)), dma, dma((4,)), dma],
        compiler_params=pltpu.CompilerParams(vmem_limit_bytes=60 * 2**20),
    )(named, spread, table, cotangent.reshape(cells, bins), coag_rate.reshape(cells // bins, bins), fwd_hi, fwd_lo,
      inv_hi, inv_lo)
    total = pl.pallas_call(
        functools.partial(return_kernel, n_lat, n_lon, cells, cap),
        out_shape=jax.ShapeDtypeStruct((cells, bins), F32),
        in_specs=[VMEM, ANY], out_specs=VMEM,
        scratch_shapes=[pltpu.VMEM((blocks, cap, bins), F32), dma((blocks,)), dma((blocks,))],
        compiler_params=pltpu.CompilerParams(
            collective_id=1, has_side_effects=True, vmem_limit_bytes=56 * 2**20),
    )(send_list.reshape(blocks * cap // bins, bins), sums)
    total = total + sums[:cells]
    return total.reshape(levels, lat_cells, lon_cells, bins)


def solution(mesh):
    grid = P(None, "lat", "lon", None)
    field = P(None, "lat", "lon")
    corner = P(None, None, "lat", "lon")
    lists = P("lat", "lon", None, None)
    body = functools.partial(on_device, mesh.shape["lat"], mesh.shape["lon"])
    return jax.shard_map(
        body, mesh=mesh, in_specs=(grid, grid, field, corner, corner, lists), out_specs=grid, check_vma=False)
```

```python
import functools

import jax
import jax.numpy as jnp
import numpy as np
from jax import lax
from jax.experimental import pallas as pl
from jax.experimental.pallas import tpu as pltpu
from jax.sharding import PartitionSpec as P

MESH = pl.DeviceIdType.MESH
F32 = jnp.float32
BF16 = jnp.bfloat16
I16 = jnp.int16
I32 = jnp.int32
SMEM = pl.BlockSpec(memory_space=pltpu.SMEM)
VMEM = pl.BlockSpec(memory_space=pltpu.VMEM)
ANY = pl.BlockSpec(memory_space=pl.ANY)
ORDER = ((0, 0), (2, 2), (0, 2), (2, 0), (1, 0), (1, 2), (0, 1), (2, 1))


def split(x):
    hi = x.astype(BF16)
    return hi, (x - hi.astype(F32)).astype(BF16)


def spectral_tables(bins):
    period = 2 * bins
    k = np.arange(bins)
    n = np.arange(bins)[:, None]
    angle = 2.0 * np.pi * (n * k % period) / period
    sine = -np.sin(angle)
    sine[:, 0] = np.cos(np.pi * np.arange(bins))
    forward = np.concatenate([np.cos(angle), sine], axis=1)
    lag = np.arange(1, bins + 1)[None, :]
    back = 2.0 * np.pi * (k[:, None] * lag % period) / period
    scale = np.where(k == 0, 1.0, 2.0)[:, None] / period
    real = np.cos(back) * scale
    imag = -np.sin(back) * scale
    imag[0] = np.cos(np.pi * lag[0]) / period
    inverse = np.concatenate([real, imag], axis=0)
    return forward.astype(np.float32), inverse.astype(np.float32)


def slot(u, v):
    b = 3 * u + v
    return b - (b > 4)


class Place:
    def __init__(self, n_lat, n_lon):
        self.lat = lax.axis_index("lat")
        self.lon = lax.axis_index("lon")
        self.n_lat = n_lat
        self.n_lon = n_lon

    def has(self, u):
        there = self.lat + u - 1
        return (there >= 0) & (there < self.n_lat)

    def at(self, u, v):
        return (self.lat + u - 1, lax.rem(self.lon + v - 1 + self.n_lon, self.n_lon))

    def greet(self):
        barrier = pltpu.get_barrier_semaphore()
        for u, v in ORDER:
            @pl.when(self.has(u))
            def _():
                pl.semaphore_signal(barrier, inc=1, device_id=self.at(u, v), device_id_type=MESH)
        count = jnp.where(self.lat > 0, 3, 0) + jnp.where(self.lat < self.n_lat - 1, 3, 0) + 2
        pl.semaphore_wait(barrier, count)


def send_kernel(n_lat, n_lon, cells, cap, slots, own, weights, departure, table, spread, named, rows, wide, flat, own_sem,
                wide_sem, flat_sem, send_sem, recv_sem):
    place = Place(n_lat, n_lon)
    place.greet()
    keep = pltpu.make_async_copy(own, table.at[pl.ds(0, cells)], own_sem)
    keep.start()

    def copy(u, v):
        b = 3 * u + v
        return pltpu.make_async_remote_copy(
            src_ref=rows.at[b], dst_ref=table.at[pl.ds(cells + slot(u, v) * cap, cap)], send_sem=send_sem.at[b],
            recv_sem=recv_sem.at[b], device_id=place.at(2 - u, 2 - v), device_id_type=MESH)

    for u, v in ORDER:
        @pl.when(place.has(2 - u))
        def _():
            b = 3 * u + v
            step = 32

            def gather(i, carry):
                for j in range(step):
                    s = i * step + j
                    rows[b, pl.ds(s, 1), :] = own[pl.ds(slots[b * cap + s], 1), :]
                return carry

            lax.fori_loop(0, cap // step, gather, 0)
            copy(u, v).start()
    corners, levels, high, long = weights.shape
    bins = own.shape[1]
    per_level = high * long * corners

    def widen(level, carry):
        values = weights[:, level]
        start = level * per_level
        for i in range(high):
            line = values[:, i, :]
            for j in range(long):
                at = pl.multiple_of(start + (i * long + j) * corners, corners)
                wide[pl.ds(at, corners), :] = jnp.broadcast_to(line[:, j:j + 1], (corners, bins))
        return carry

    lax.fori_loop(0, levels, widen, 0)
    store = pltpu.make_async_copy(wide, spread, wide_sem)
    store.start()
    packs = bins // long
    mine = lax.broadcasted_iota(I32, (high, bins), 1) // long == lax.broadcasted_iota(I32, (high, bins), 0) % packs

    def flatten(k, carry):
        lines = []
        for level in range(levels):
            value = departure[k, level]
            value = jnp.where(value < cells + 5 * cap, value, value - cap)
            value = jnp.where(mine, jnp.concatenate([value] * packs, axis=1), 0)
            lines += [jnp.sum(value[h:h + packs], axis=0, keepdims=True) for h in range(0, high, packs)]
        count = len(lines)
        flat[pl.ds(pl.multiple_of(k * count, count), count), :] = jnp.concatenate(lines, axis=0)
        return carry

    lax.fori_loop(0, corners, flatten, 0)
    note = pltpu.make_async_copy(flat, named, flat_sem)
    note.start()
    keep.wait()
    store.wait()
    note.wait()
    for u, v in ORDER:
        @pl.when(place.has(u))
        def _():
            copy(u, v).wait_recv()

        @pl.when(place.has(2 - u))
        def _():
            copy(u, v).wait_send()


def cell_kernel(cells, corners, *refs):
    (named, spread, table_hbm, cot, rate, fwd_hi, fwd_lo, inv_hi, inv_lo, sums), refs = refs[:10], refs[10:]
    (table, state, wide), refs = refs[:3], refs[3:]
    accs, refs = refs[:corners], refs[corners:]
    index, (index_sem, table_sem, wide_sem, out_sem) = refs[:corners], refs[corners:]
    entries, bins = table.shape
    load = pltpu.make_async_copy(table_hbm, table, table_sem)
    load.start()
    loads = [pltpu.make_async_copy(named.at[pl.ds(k * cells, cells)], index[k], index_sem.at[k]) for k in range(corners)]
    for copy in loads:
        copy.start()
    parts = 4
    part = cells // parts
    wides = []
    for p in range(parts):
        here = pl.ds(p * part * corners, part * corners)
        wides.append(pltpu.make_async_copy(spread.at[here], wide.at[here], wide_sem.at[p]))
        wides[p].start()
    for copy in loads:
        copy.wait()
    load.wait()
    step = 16
    clear = entries * step // cells

    def gather(i, carry):
        for j in range(step):
            a = i * step + j
            total = None
            for k in range(corners):
                row = table[pl.ds(index[k][a], 1), :] * wide[pl.ds(a * corners + k, 1), :]
                total = row if total is None else total + row
            state[pl.ds(a, 1), :] = total
        for acc in accs:
            acc[pl.ds(pl.multiple_of(i * clear, clear), clear), :] = jnp.zeros((clear, bins), F32)
        return carry

    for p in range(parts):
        wides[p].wait()
        lax.fori_loop(p * part // step, (p + 1) * part // step, gather, 0)
    levels, high, long = rate.shape
    tile = high * long
    first = lax.broadcasted_iota(I32, (tile, bins), 1) == 0
    diagonal = lax.broadcasted_iota(I32, (tile, long), 0) % long == lax.broadcasted_iota(I32, (tile, long), 1)

    def dot3(x, hi, lo):
        xh, xl = split(x)
        out = jnp.dot(xh, hi[...], preferred_element_type=F32)
        out += jnp.dot(xl, hi[...], preferred_element_type=F32)
        return out + jnp.dot(xh, lo[...], preferred_element_type=F32)

    def react(i, carry):
        here = pl.ds(pl.multiple_of(i * tile, tile), tile)
        t = state[here, :]
        c = cot[here, :]
        ts = dot3(t, fwd_hi, fwd_lo)
        cs = dot3(c, fwd_hi, fwd_lo)
        ta, tb, ca, cb = ts[:, :bins], ts[:, bins:], cs[:, :bins], cs[:, bins:]
        both = tb * cb
        real = ta * ca + jnp.where(first, 0.0, both)
        imag = jnp.where(first, both, ta * cb - tb * ca)
        lagged = dot3(jnp.concatenate([real, imag], axis=1), inv_hi, inv_lo)
        totals = jnp.sum(t, axis=1, keepdims=True)
        weighed = jnp.sum(t * c, axis=1, keepdims=True)
        lines = rate[i]
        spread_lines = jnp.concatenate([jnp.broadcast_to(lines[h:h + 1, :], (long, long)) for h in range(high)], axis=0)
        speed = jnp.sum(jnp.where(diagonal, spread_lines, 0.0), axis=1, keepdims=True)
        state[here, :] = c + speed * (lagged - totals * c - weighed)
        return carry

    lax.fori_loop(0, cells // tile, react, 0)

    def scatter(i, carry):
        for j in range(step):
            a = i * step + j
            row = state[pl.ds(a, 1), :]
            at = [pl.ds(index[k][a], 1) for k in range(corners)]
            new = [accs[k][at[k], :] + row * wide[pl.ds(a * corners + k, 1), :] for k in range(corners)]
            for k in range(corners):
                accs[k][at[k], :] = new[k]
        return carry

    lax.fori_loop(0, cells // step, scatter, 0)
    chunk = 512

    def merge(i, carry):
        here = pl.ds(pl.multiple_of(i * chunk, chunk), chunk)
        total = accs[0][here, :]
        for acc in accs[1:]:
            total = total + acc[here, :]
        table[here, :] = total
        pltpu.make_async_copy(table.at[here], sums.at[here], out_sem).start()
        return carry

    lax.fori_loop(0, entries // chunk, merge, 0)
    pltpu.make_async_copy(table, sums, out_sem).wait()


def return_kernel(n_lat, n_lon, cells, cap, slots, sums, out, back, send_sem, recv_sem):
    place = Place(n_lat, n_lon)
    place.greet()

    def copy(u, v):
        b = 3 * u + v
        return pltpu.make_async_remote_copy(
            src_ref=sums.at[pl.ds(cells + slot(u, v) * cap, cap)], dst_ref=back.at[b], send_sem=send_sem.at[b],
            recv_sem=recv_sem.at[b], device_id=place.at(u, v), device_id_type=MESH)

    def send(pairs):
        for u, v in pairs:
            @pl.when(place.has(u))
            def _():
                copy(u, v).start()

    def sent(pairs):
        for u, v in pairs:
            @pl.when(place.has(u))
            def _():
                copy(u, v).wait_send()

    tile = 256
    bins = out.shape[1]
    number = lax.broadcasted_iota(I32, (tile, bins), 0).astype(I16)

    def collect(pairs):
        for u, v in pairs:
            @pl.when(place.has(2 - u))
            def _():
                b = 3 * u + v
                copy(u, v).wait_recv()
                rows = jnp.concatenate(split(back[b]), axis=1)
                lines = cap // bins
                named = [slots[pl.ds(b * lines + q, 1), :] for q in range(lines)]

                def add(i, carry):
                    here = pl.ds(pl.multiple_of(i * tile, tile), tile)
                    hits = [(line - i * tile).astype(I16) == number for line in named]
                    pick = jnp.concatenate(
                        [jnp.where(hit, jnp.ones((), BF16), jnp.zeros((), BF16)) for hit in hits], axis=1)
                    got = jnp.dot(pick, rows, preferred_element_type=F32)
                    out[here, :] += got[:, :bins] + got[:, bins:]
                    return carry

                lax.fori_loop(0, cells // tile, add, 0)

    send(ORDER[:4])
    send(ORDER[6:])
    out[...] = jnp.zeros_like(out)
    collect(ORDER[6:])
    sent(ORDER[:2])
    send(ORDER[4:6])
    collect(ORDER[:6])
    sent(ORDER[2:])


def on_device(n_lat, n_lon, concentration, cotangent, coag_rate, weights, departure, send_list):
    levels, lat_cells, lon_cells, bins = concentration.shape
    cells = levels * lat_cells * lon_cells
    blocks, cap = send_list.shape[2:]
    corners = departure.shape[0]
    entries = cells + (blocks - 1) * cap
    own = concentration.reshape(cells, bins)
    dma = pltpu.SemaphoreType.DMA
    table, spread, named = pl.pallas_call(
        functools.partial(send_kernel, n_lat, n_lon, cells, cap),
        out_shape=[jax.ShapeDtypeStruct((entries, bins), F32), jax.ShapeDtypeStruct((cells * corners, bins), F32),
                   jax.ShapeDtypeStruct((corners * cells // bins, bins), I32)],
        in_specs=[SMEM, VMEM, VMEM, VMEM], out_specs=[ANY, ANY, ANY],
        scratch_shapes=[pltpu.VMEM((blocks, cap, bins), F32), pltpu.VMEM((cells * corners, bins), F32),
                        pltpu.VMEM((corners * cells // bins, bins), I32), dma, dma, dma, dma((blocks,)), dma((blocks,))],
        compiler_params=pltpu.CompilerParams(
            collective_id=0, has_side_effects=True, vmem_limit_bytes=56 * 2**20),
    )(send_list.reshape(blocks * cap), own, weights, departure)
    forward, inverse = spectral_tables(bins)
    fwd_hi, fwd_lo = split(jnp.asarray(forward))
    inv_hi, inv_lo = split(jnp.asarray(inverse))
    sums = pl.pallas_call(
        functools.partial(cell_kernel, cells, corners),
        out_shape=jax.ShapeDtypeStruct((entries, bins), F32),
        in_specs=[ANY, ANY, ANY] + [VMEM] * 6, out_specs=ANY,
        scratch_shapes=[pltpu.VMEM((entries, bins), F32), pltpu.VMEM((cells, bins), F32),
                        pltpu.VMEM((cells * corners, bins), F32)]
        + [pltpu.VMEM((entries, bins), F32)] * corners + [pltpu.SMEM((cells,), I32)] * corners
        + [dma((corners,)), dma, dma((4,)), dma],
        compiler_params=pltpu.CompilerParams(vmem_limit_bytes=60 * 2**20),
    )(named.reshape(-1), spread, table, cotangent.reshape(cells, bins), coag_rate, fwd_hi, fwd_lo,
      inv_hi, inv_lo)
    total = pl.pallas_call(
        functools.partial(return_kernel, n_lat, n_lon, cells, cap),
        out_shape=jax.ShapeDtypeStruct((cells, bins), F32),
        in_specs=[VMEM, ANY], out_specs=VMEM,
        scratch_shapes=[pltpu.VMEM((blocks, cap, bins), F32), dma((blocks,)), dma((blocks,))],
        compiler_params=pltpu.CompilerParams(
            collective_id=1, has_side_effects=True, vmem_limit_bytes=56 * 2**20),
    )(send_list.reshape(blocks * cap // bins, bins), sums)
    total = total + sums[:cells]
    return total.reshape(levels, lat_cells, lon_cells, bins)


def solution(mesh):
    grid = P(None, "lat", "lon", None)
    field = P(None, "lat", "lon")
    corner = P(None, None, "lat", "lon")
    lists = P("lat", "lon", None, None)
    body = functools.partial(on_device, mesh.shape["lat"], mesh.shape["lon"])
    return jax.shard_map(
        body, mesh=mesh, in_specs=(grid, grid, field, corner, corner, lists), out_specs=grid, check_vma=False)
```

```python
import functools

import jax
import jax.numpy as jnp
import numpy as np
from jax import lax
from jax.experimental import pallas as pl
from jax.experimental.pallas import tpu as pltpu
from jax.sharding import PartitionSpec as P

MESH = pl.DeviceIdType.MESH
F32 = jnp.float32
BF16 = jnp.bfloat16
I16 = jnp.int16
I32 = jnp.int32
SMEM = pl.BlockSpec(memory_space=pltpu.SMEM)
VMEM = pl.BlockSpec(memory_space=pltpu.VMEM)
ANY = pl.BlockSpec(memory_space=pl.ANY)
FIRST = ((1, 0), (1, 2))
CORNER = ((0, 0), (2, 2), (0, 2), (2, 0))
REST = ((0, 1), (2, 1))
NEXT = CORNER + REST
BACK = CORNER + FIRST + REST

PARTS = 8


def split(x):
    hi = x.astype(BF16)
    return hi, (x - hi.astype(F32)).astype(BF16)


def spectral_tables(bins):
    period = 2 * bins
    k = np.arange(bins)
    n = np.arange(bins)[:, None]
    angle = 2.0 * np.pi * (n * k % period) / period
    sine = -np.sin(angle)
    sine[:, 0] = np.cos(np.pi * np.arange(bins))
    forward = np.concatenate([np.cos(angle), sine], axis=1)
    lag = np.arange(1, bins + 1)[None, :]
    back = 2.0 * np.pi * (k[:, None] * lag % period) / period
    scale = np.where(k == 0, 1.0, 2.0)[:, None] / period
    real = np.cos(back) * scale
    imag = -np.sin(back) * scale
    imag[0] = np.cos(np.pi * lag[0]) / period
    inverse = np.concatenate([real, imag], axis=0)
    return forward.astype(np.float32), inverse.astype(np.float32)


def slot(u, v):
    b = 3 * u + v
    return b - (b > 4)


class Place:
    def __init__(self, n_lat, n_lon):
        self.lat = lax.axis_index("lat")
        self.lon = lax.axis_index("lon")
        self.n_lat = n_lat
        self.n_lon = n_lon

    def has(self, u):
        there = self.lat + u - 1
        return (there >= 0) & (there < self.n_lat)

    def at(self, u, v):
        return (self.lat + u - 1, lax.rem(self.lon + v - 1 + self.n_lon, self.n_lon))

    def greet(self):
        barrier = pltpu.get_barrier_semaphore()
        for u, v in FIRST + NEXT:
            @pl.when(self.has(u))
            def _():
                pl.semaphore_signal(barrier, inc=1, device_id=self.at(u, v), device_id_type=MESH)
        count = jnp.where(self.lat > 0, 3, 0) + jnp.where(self.lat < self.n_lat - 1, 3, 0) + 2
        pl.semaphore_wait(barrier, count)


def send_kernel(n_lat, n_lon, cells, cap, slots_in, own_in, weights_in, departure_in, table, spread, named, slots, own,
                weights, departure, rows, wide, flat, in_sem, own_sem, wide_sem, flat_sem, send_sem, recv_sem, half_send,
                half_recv):
    pairs = ((slots_in, slots), (own_in, own), (weights_in, weights), (departure_in, departure))
    loads = [pltpu.make_async_copy(source, target, in_sem.at[n]) for n, (source, target) in enumerate(pairs)]
    for load in loads:
        load.start()
    place = Place(n_lat, n_lon)
    place.greet()
    keep = pltpu.make_async_copy(own_in, table.at[pl.ds(0, cells)], own_sem)
    loads[0].wait()
    loads[1].wait()

    def copy(u, v):
        b = 3 * u + v
        return pltpu.make_async_remote_copy(
            src_ref=rows.at[b], dst_ref=table.at[pl.ds(cells + slot(u, v) * cap, cap)], send_sem=send_sem.at[b],
            recv_sem=recv_sem.at[b], device_id=place.at(2 - u, 2 - v), device_id_type=MESH)

    half = cap // 2

    def half_copy(u, v, h):
        b = 3 * u + v
        sem = 2 * (v // 2) + h
        return pltpu.make_async_remote_copy(
            src_ref=rows.at[b, pl.ds(h * half, half)],
            dst_ref=table.at[pl.ds(cells + slot(u, v) * cap + h * half, half)], send_sem=half_send.at[sem],
            recv_sem=half_recv.at[sem], device_id=place.at(2 - u, 2 - v), device_id_type=MESH)

    def pick(b, low, count):
        step = 32

        def gather(i, carry):
            for j in range(step):
                s = low + i * step + j
                rows[b, pl.ds(s, 1), :] = own[pl.ds(slots[b * cap + s], 1), :]
            return carry

        lax.fori_loop(0, count // step, gather, 0)

    for h in range(2):
        for u, v in FIRST:
            pick(3 * u + v, h * half, half)
            half_copy(u, v, h).start()
    for u, v in NEXT:
        @pl.when(place.has(2 - u))
        def _():
            pick(3 * u + v, 0, cap)
            copy(u, v).start()
    keep.start()
    loads[2].wait()
    loads[3].wait()
    corners, levels, high, long = weights.shape
    bins = own.shape[1]
    per_level = high * long * corners

    def widen(level, carry):
        values = weights[:, level]
        start = level * per_level
        for i in range(high):
            line = values[:, i, :]
            for j in range(long):
                at = pl.multiple_of(start + (i * long + j) * corners, corners)
                wide[pl.ds(at, corners), :] = jnp.broadcast_to(line[:, j:j + 1], (corners, bins))
        return carry

    lax.fori_loop(0, levels, widen, 0)
    store = pltpu.make_async_copy(wide, spread, wide_sem)
    store.start()
    packs = bins // long
    mine = lax.broadcasted_iota(I32, (high, bins), 1) // long == lax.broadcasted_iota(I32, (high, bins), 0) % packs

    def flatten(k, carry):
        lines = []
        for level in range(levels):
            value = departure[k, level]
            value = jnp.where(value < cells + 5 * cap, value, value - cap)
            value = jnp.where(mine, jnp.concatenate([value] * packs, axis=1), 0)
            lines += [jnp.sum(value[h:h + packs], axis=0, keepdims=True) for h in range(0, high, packs)]
        count = len(lines)
        flat[pl.ds(pl.multiple_of(k * count, count), count), :] = jnp.concatenate(lines, axis=0)
        return carry

    lax.fori_loop(0, corners, flatten, 0)
    note = pltpu.make_async_copy(flat, named, flat_sem)
    note.start()
    keep.wait()
    store.wait()
    note.wait()
    for h in range(2):
        for u, v in FIRST:
            half_copy(u, v, h).wait_recv()
            half_copy(u, v, h).wait_send()
    for u, v in NEXT:
        @pl.when(place.has(u))
        def _():
            copy(u, v).wait_recv()

        @pl.when(place.has(2 - u))
        def _():
            copy(u, v).wait_send()


def cell_kernel(cells, corners, *refs):
    (named, spread, table_hbm), later_in, sums, refs = refs[:3], refs[3:9], refs[9], refs[10:]
    (table, state, wide), later, refs = refs[:3], refs[3:9], refs[9:]
    cot, rate, fwd_hi, fwd_lo, inv_hi, inv_lo = later
    accs, refs = refs[:corners], refs[corners:]
    index, (index_sem, table_sem, wide_sem, later_sem, out_sem) = refs[:corners], refs[corners:]
    entries, bins = table.shape
    load = pltpu.make_async_copy(table_hbm, table, table_sem)
    load.start()
    loads = [pltpu.make_async_copy(named.at[pl.ds(k * cells, cells)], index[k], index_sem.at[k]) for k in range(corners)]
    for copy in loads:
        copy.start()
    part = cells // PARTS

    def wide_copy(p):
        here = pl.ds(pl.multiple_of(p * part * corners, part * corners), part * corners)
        return pltpu.make_async_copy(spread.at[here], wide.at[here], wide_sem.at[p])

    for p in range(2):
        wide_copy(p).start()
    for copy in loads:
        copy.wait()
    load.wait()
    for p in range(2, PARTS):
        wide_copy(p).start()
    laters = [pltpu.make_async_copy(source, target, later_sem.at[n])
              for n, (source, target) in enumerate(zip(later_in, later))]
    for copy in laters:
        copy.start()
    step = 16
    clear = entries * step // cells

    def gather(i, carry):
        for j in range(step):
            a = i * step + j
            total = None
            for k in range(corners):
                row = table[pl.ds(index[k][a], 1), :] * wide[pl.ds(a * corners + k, 1), :]
                total = row if total is None else total + row
            state[pl.ds(a, 1), :] = total
        for acc in accs:
            acc[pl.ds(pl.multiple_of(i * clear, clear), clear), :] = jnp.zeros((clear, bins), F32)
        return carry

    def next_part(p, carry):
        wide_copy(p).wait()
        lax.fori_loop(p * (part // step), (p + 1) * (part // step), gather, 0)
        return carry

    lax.fori_loop(0, PARTS, next_part, 0)
    for copy in laters:
        copy.wait()
    levels, high, long = rate.shape
    tile = high * long
    first = lax.broadcasted_iota(I32, (tile, bins), 1) == 0
    diagonal = lax.broadcasted_iota(I32, (tile, long), 0) % long == lax.broadcasted_iota(I32, (tile, long), 1)

    def dot3(x, hi, lo):
        xh, xl = split(x)
        out = jnp.dot(xh, hi[...], preferred_element_type=F32)
        out += jnp.dot(xl, hi[...], preferred_element_type=F32)
        return out + jnp.dot(xh, lo[...], preferred_element_type=F32)

    def react(i, carry):
        here = pl.ds(pl.multiple_of(i * tile, tile), tile)
        t = state[here, :]
        c = cot[here, :]
        ts = dot3(t, fwd_hi, fwd_lo)
        cs = dot3(c, fwd_hi, fwd_lo)
        ta, tb, ca, cb = ts[:, :bins], ts[:, bins:], cs[:, :bins], cs[:, bins:]
        both = tb * cb
        real = ta * ca + jnp.where(first, 0.0, both)
        imag = jnp.where(first, both, ta * cb - tb * ca)
        lagged = dot3(jnp.concatenate([real, imag], axis=1), inv_hi, inv_lo)
        totals = jnp.sum(t, axis=1, keepdims=True)
        weighed = jnp.sum(t * c, axis=1, keepdims=True)
        lines = rate[i]
        spread_lines = jnp.concatenate([jnp.broadcast_to(lines[h:h + 1, :], (long, long)) for h in range(high)], axis=0)
        speed = jnp.sum(jnp.where(diagonal, spread_lines, 0.0), axis=1, keepdims=True)
        state[here, :] = c + speed * (lagged - totals * c - weighed)
        return carry

    lax.fori_loop(0, cells // tile, react, 0)

    def scatter(i, carry):
        for j in range(step):
            a = i * step + j
            row = state[pl.ds(a, 1), :]
            at = [pl.ds(index[k][a], 1) for k in range(corners)]
            new = [accs[k][at[k], :] + row * wide[pl.ds(a * corners + k, 1), :] for k in range(corners)]
            for k in range(corners):
                accs[k][at[k], :] = new[k]
        return carry

    lax.fori_loop(0, cells // step, scatter, 0)
    chunk = 512

    def merge(i, carry):
        here = pl.ds(pl.multiple_of(i * chunk, chunk), chunk)
        total = accs[0][here, :]
        for acc in accs[1:]:
            total = total + acc[here, :]
        table[here, :] = total
        pltpu.make_async_copy(table.at[here], sums.at[here], out_sem).start()
        return carry

    lax.fori_loop(0, entries // chunk, merge, 0)
    pltpu.make_async_copy(table, sums, out_sem).wait()


def return_kernel(n_lat, n_lon, cells, cap, slots_in, sums, out, slots, back, slots_sem, own_sem, send_sem, recv_sem):
    place = Place(n_lat, n_lon)
    load = pltpu.make_async_copy(slots_in, slots, slots_sem)
    load.start()
    place.greet()

    def copy(u, v):
        b = 3 * u + v
        return pltpu.make_async_remote_copy(
            src_ref=sums.at[pl.ds(cells + slot(u, v) * cap, cap)], dst_ref=back.at[b], send_sem=send_sem.at[b],
            recv_sem=recv_sem.at[b], device_id=place.at(u, v), device_id_type=MESH)

    def send(pairs):
        for u, v in pairs:
            @pl.when(place.has(u))
            def _():
                copy(u, v).start()

    def sent(pairs):
        for u, v in pairs:
            @pl.when(place.has(u))
            def _():
                copy(u, v).wait_send()

    tile = 256
    bins = out.shape[1]
    number = lax.broadcasted_iota(I32, (tile, bins), 0).astype(I16)

    def collect(pairs):
        for u, v in pairs:
            @pl.when(place.has(2 - u))
            def _():
                b = 3 * u + v
                copy(u, v).wait_recv()
                rows = jnp.concatenate(split(back[b]), axis=1)
                lines = cap // bins
                named = [slots[pl.ds(b * lines + q, 1), :] for q in range(lines)]

                def add(i, carry):
                    here = pl.ds(pl.multiple_of(i * tile, tile), tile)
                    hits = [(line - i * tile).astype(I16) == number for line in named]
                    pick = jnp.concatenate(
                        [jnp.where(hit, jnp.ones((), BF16), jnp.zeros((), BF16)) for hit in hits], axis=1)
                    got = jnp.dot(pick, rows, preferred_element_type=F32)
                    out[here, :] += got[:, :bins] + got[:, bins:]
                    return carry

                lax.fori_loop(0, cells // tile, add, 0)

    send(BACK[:4])
    send(BACK[6:])
    keep = pltpu.make_async_copy(sums.at[pl.ds(0, cells)], out, own_sem)
    keep.start()
    load.wait()
    keep.wait()
    collect(BACK[6:])
    sent(BACK[:2])
    send(BACK[4:6])
    collect(BACK[:6])
    sent(BACK[2:])


def on_device(n_lat, n_lon, concentration, cotangent, coag_rate, weights, departure, send_list):
    levels, lat_cells, lon_cells, bins = concentration.shape
    cells = levels * lat_cells * lon_cells
    blocks, cap = send_list.shape[2:]
    corners = departure.shape[0]
    entries = cells + (blocks - 1) * cap
    own = concentration.reshape(cells, bins)
    dma = pltpu.SemaphoreType.DMA
    table, spread, named = pl.pallas_call(
        functools.partial(send_kernel, n_lat, n_lon, cells, cap),
        out_shape=[jax.ShapeDtypeStruct((entries, bins), F32), jax.ShapeDtypeStruct((cells * corners, bins), F32),
                   jax.ShapeDtypeStruct((corners * cells // bins, bins), I32)],
        in_specs=[ANY] * 4, out_specs=[ANY, ANY, ANY],
        scratch_shapes=[pltpu.SMEM((blocks * cap,), I32), pltpu.VMEM((cells, bins), F32),
                        pltpu.VMEM(weights.shape, F32), pltpu.VMEM(departure.shape, I32),
                        pltpu.VMEM((blocks, cap, bins), F32), pltpu.VMEM((cells * corners, bins), F32),
                        pltpu.VMEM((corners * cells // bins, bins), I32), dma((4,)), dma, dma, dma, dma((blocks,)), dma((blocks,)),
                        dma((4,)), dma((4,))],
        compiler_params=pltpu.CompilerParams(
            collective_id=0, has_side_effects=True, vmem_limit_bytes=60 * 2**20),
    )(send_list.reshape(blocks * cap), own, weights, departure)
    forward, inverse = spectral_tables(bins)
    fwd_hi, fwd_lo = split(jnp.asarray(forward))
    inv_hi, inv_lo = split(jnp.asarray(inverse))
    sums = pl.pallas_call(
        functools.partial(cell_kernel, cells, corners),
        out_shape=jax.ShapeDtypeStruct((entries, bins), F32),
        in_specs=[ANY] * 9, out_specs=ANY,
        scratch_shapes=[pltpu.VMEM((entries, bins), F32), pltpu.VMEM((cells, bins), F32),
                        pltpu.VMEM((cells * corners, bins), F32), pltpu.VMEM((cells, bins), F32),
                        pltpu.VMEM(coag_rate.shape, F32)]
        + [pltpu.VMEM(part.shape, BF16) for part in (fwd_hi, fwd_lo, inv_hi, inv_lo)]
        + [pltpu.VMEM((entries, bins), F32)] * corners + [pltpu.SMEM((cells,), I32)] * corners
        + [dma((corners,)), dma, dma((PARTS,)), dma((6,)), dma],
        compiler_params=pltpu.CompilerParams(vmem_limit_bytes=60 * 2**20),
    )(named.reshape(-1), spread, table, cotangent.reshape(cells, bins), coag_rate, fwd_hi, fwd_lo,
      inv_hi, inv_lo)
    total = pl.pallas_call(
        functools.partial(return_kernel, n_lat, n_lon, cells, cap),
        out_shape=jax.ShapeDtypeStruct((cells, bins), F32),
        in_specs=[ANY, ANY], out_specs=VMEM,
        scratch_shapes=[pltpu.VMEM((blocks * cap // bins, bins), I32), pltpu.VMEM((blocks, cap, bins), F32), dma, dma,
                        dma((blocks,)), dma((blocks,))],
        compiler_params=pltpu.CompilerParams(
            collective_id=1, has_side_effects=True, vmem_limit_bytes=60 * 2**20),
    )(send_list.reshape(blocks * cap // bins, bins), sums)
    return total.reshape(levels, lat_cells, lon_cells, bins)


def solution(mesh):
    grid = P(None, "lat", "lon", None)
    field = P(None, "lat", "lon")
    corner = P(None, None, "lat", "lon")
    lists = P("lat", "lon", None, None)
    body = functools.partial(on_device, mesh.shape["lat"], mesh.shape["lon"])
    return jax.shard_map(
        body, mesh=mesh, in_specs=(grid, grid, field, corner, corner, lists), out_specs=grid, check_vma=False)
```

```python
import functools

import jax
import jax.numpy as jnp
import numpy as np
from jax import lax
from jax.experimental import pallas as pl
from jax.experimental.pallas import tpu as pltpu
from jax.sharding import PartitionSpec as P

MESH = pl.DeviceIdType.MESH
F32 = jnp.float32
BF16 = jnp.bfloat16
I16 = jnp.int16
I32 = jnp.int32
SMEM = pl.BlockSpec(memory_space=pltpu.SMEM)
VMEM = pl.BlockSpec(memory_space=pltpu.VMEM)
ANY = pl.BlockSpec(memory_space=pl.ANY)
FIRST = ((1, 0), (1, 2))
CORNER = ((0, 0), (2, 2), (0, 2), (2, 0))
REST = ((0, 1), (2, 1))
NEXT = CORNER + REST
BACK = CORNER + FIRST + REST

PARTS = 8


def split(x):
    hi = x.astype(BF16)
    return hi, (x - hi.astype(F32)).astype(BF16)


def spectral_tables(bins):
    period = 2 * bins
    k = np.arange(bins)
    n = np.arange(bins)[:, None]
    angle = 2.0 * np.pi * (n * k % period) / period
    sine = -np.sin(angle)
    sine[:, 0] = np.cos(np.pi * np.arange(bins))
    forward = np.concatenate([np.cos(angle), sine], axis=1)
    lag = np.arange(1, bins + 1)[None, :]
    back = 2.0 * np.pi * (k[:, None] * lag % period) / period
    scale = np.where(k == 0, 1.0, 2.0)[:, None] / period
    real = np.cos(back) * scale
    imag = -np.sin(back) * scale
    imag[0] = np.cos(np.pi * lag[0]) / period
    inverse = np.concatenate([real, imag], axis=0)
    return forward.astype(np.float32), inverse.astype(np.float32)


def slot(u, v):
    b = 3 * u + v
    return b - (b > 4)


class Place:
    def __init__(self, n_lat, n_lon):
        self.lat = lax.axis_index("lat")
        self.lon = lax.axis_index("lon")
        self.n_lat = n_lat
        self.n_lon = n_lon

    def has(self, u):
        there = self.lat + u - 1
        return (there >= 0) & (there < self.n_lat)

    def at(self, u, v):
        return (self.lat + u - 1, lax.rem(self.lon + v - 1 + self.n_lon, self.n_lon))

    def greet(self):
        barrier = pltpu.get_barrier_semaphore()
        for u, v in FIRST + NEXT:
            @pl.when(self.has(u))
            def _():
                pl.semaphore_signal(barrier, inc=1, device_id=self.at(u, v), device_id_type=MESH)
        count = jnp.where(self.lat > 0, 3, 0) + jnp.where(self.lat < self.n_lat - 1, 3, 0) + 2
        pl.semaphore_wait(barrier, count)


def send_kernel(n_lat, n_lon, cells, cap, slots_in, own_in, weights_in, departure_in, table, spread, named, slots, own,
                weights, departure, rows, wide, flat, in_sem, own_sem, wide_sem, flat_sem, send_sem, recv_sem, half_send,
                half_recv):
    pairs = ((slots_in, slots), (own_in, own), (weights_in, weights), (departure_in, departure))
    loads = [pltpu.make_async_copy(source, target, in_sem.at[n]) for n, (source, target) in enumerate(pairs)]
    for load in loads:
        load.start()
    place = Place(n_lat, n_lon)
    place.greet()
    keep = pltpu.make_async_copy(own, table.at[pl.ds(0, cells)], own_sem)
    loads[0].wait()
    loads[1].wait()

    def copy(u, v):
        b = 3 * u + v
        return pltpu.make_async_remote_copy(
            src_ref=rows.at[b], dst_ref=table.at[pl.ds(cells + slot(u, v) * cap, cap)], send_sem=send_sem.at[b],
            recv_sem=recv_sem.at[b], device_id=place.at(2 - u, 2 - v), device_id_type=MESH)

    half = cap // 2

    def half_copy(u, v, h):
        b = 3 * u + v
        sem = 2 * (v // 2) + h
        return pltpu.make_async_remote_copy(
            src_ref=rows.at[b, pl.ds(h * half, half)],
            dst_ref=table.at[pl.ds(cells + slot(u, v) * cap + h * half, half)], send_sem=half_send.at[sem],
            recv_sem=half_recv.at[sem], device_id=place.at(2 - u, 2 - v), device_id_type=MESH)

    def pick(b, low, count):
        step = 32

        def gather(i, carry):
            for j in range(step):
                s = low + i * step + j
                rows[b, pl.ds(s, 1), :] = own[pl.ds(slots[b * cap + s], 1), :]
            return carry

        lax.fori_loop(0, count // step, gather, 0)

    for h in range(2):
        for u, v in FIRST:
            pick(3 * u + v, h * half, half)
            half_copy(u, v, h).start()
    for u, v in NEXT:
        @pl.when(place.has(2 - u))
        def _():
            pick(3 * u + v, 0, cap)
            copy(u, v).start()
    keep.start()
    loads[2].wait()
    loads[3].wait()
    corners, levels, high, long = weights.shape
    bins = own.shape[1]
    per_level = high * long * corners

    def widen(level, carry):
        values = weights[:, level]
        start = level * per_level
        for i in range(high):
            line = values[:, i, :]
            for j in range(long):
                at = pl.multiple_of(start + (i * long + j) * corners, corners)
                wide[pl.ds(at, corners), :] = jnp.broadcast_to(line[:, j:j + 1], (corners, bins))
        return carry

    lax.fori_loop(0, levels, widen, 0)
    store = pltpu.make_async_copy(wide, spread, wide_sem)
    store.start()
    packs = bins // long
    mine = lax.broadcasted_iota(I32, (high, bins), 1) // long == lax.broadcasted_iota(I32, (high, bins), 0) % packs

    def flatten(k, carry):
        lines = []
        for level in range(levels):
            value = departure[k, level]
            value = jnp.where(value < cells + 5 * cap, value, value - cap)
            value = jnp.where(mine, jnp.concatenate([value] * packs, axis=1), 0)
            lines += [jnp.sum(value[h:h + packs], axis=0, keepdims=True) for h in range(0, high, packs)]
        count = len(lines)
        flat[pl.ds(pl.multiple_of(k * count, count), count), :] = jnp.concatenate(lines, axis=0)
        return carry

    lax.fori_loop(0, corners, flatten, 0)
    note = pltpu.make_async_copy(flat, named, flat_sem)
    note.start()
    keep.wait()
    store.wait()
    note.wait()
    for h in range(2):
        for u, v in FIRST:
            half_copy(u, v, h).wait_recv()
            half_copy(u, v, h).wait_send()
    for u, v in NEXT:
        @pl.when(place.has(u))
        def _():
            copy(u, v).wait_recv()

        @pl.when(place.has(2 - u))
        def _():
            copy(u, v).wait_send()


def cell_kernel(cells, corners, *refs):
    (named, spread, table_hbm), later_in, sums, refs = refs[:3], refs[3:9], refs[9], refs[10:]
    (table, state, wide), later, refs = refs[:3], refs[3:9], refs[9:]
    cot, rate, fwd_hi, fwd_lo, inv_hi, inv_lo = later
    accs, refs = refs[:corners], refs[corners:]
    index, (index_sem, table_sem, wide_sem, later_sem, out_sem) = refs[:corners], refs[corners:]
    entries, bins = table.shape
    load = pltpu.make_async_copy(table_hbm, table, table_sem)
    load.start()
    loads = [pltpu.make_async_copy(named.at[pl.ds(k * cells, cells)], index[k], index_sem.at[k]) for k in range(corners)]
    for copy in loads:
        copy.start()
    part = cells // PARTS

    def wide_copy(p):
        here = pl.ds(pl.multiple_of(p * part * corners, part * corners), part * corners)
        return pltpu.make_async_copy(spread.at[here], wide.at[here], wide_sem.at[p])

    for p in range(2):
        wide_copy(p).start()
    for copy in loads:
        copy.wait()
    load.wait()
    for p in range(2, PARTS):
        wide_copy(p).start()
    laters = [pltpu.make_async_copy(source, target, later_sem.at[n])
              for n, (source, target) in enumerate(zip(later_in, later))]
    for copy in laters:
        copy.start()
    step = 16
    clear = entries * step // cells

    def gather(i, carry):
        for j in range(step):
            a = i * step + j
            total = None
            for k in range(corners):
                row = table[pl.ds(index[k][a], 1), :] * wide[pl.ds(a * corners + k, 1), :]
                total = row if total is None else total + row
            state[pl.ds(a, 1), :] = total
        for acc in accs:
            acc[pl.ds(pl.multiple_of(i * clear, clear), clear), :] = jnp.zeros((clear, bins), F32)
        return carry

    def next_part(p, carry):
        wide_copy(p).wait()
        lax.fori_loop(p * (part // step), (p + 1) * (part // step), gather, 0)
        return carry

    lax.fori_loop(0, PARTS, next_part, 0)
    for copy in laters:
        copy.wait()
    levels, high, long = rate.shape
    tile = high * long
    first = lax.broadcasted_iota(I32, (tile, bins), 1) == 0
    diagonal = lax.broadcasted_iota(I32, (tile, long), 0) % long == lax.broadcasted_iota(I32, (tile, long), 1)

    def dot3(x, hi, lo):
        xh, xl = split(x)
        out = jnp.dot(xh, hi[...], preferred_element_type=F32)
        out += jnp.dot(xl, hi[...], preferred_element_type=F32)
        return out + jnp.dot(xh, lo[...], preferred_element_type=F32)

    def react(i, carry):
        here = pl.ds(pl.multiple_of(i * tile, tile), tile)
        t = state[here, :]
        c = cot[here, :]
        ts = dot3(t, fwd_hi, fwd_lo)
        cs = dot3(c, fwd_hi, fwd_lo)
        ta, tb, ca, cb = ts[:, :bins], ts[:, bins:], cs[:, :bins], cs[:, bins:]
        both = tb * cb
        real = ta * ca + jnp.where(first, 0.0, both)
        imag = jnp.where(first, both, ta * cb - tb * ca)
        lagged = dot3(jnp.concatenate([real, imag], axis=1), inv_hi, inv_lo)
        totals = jnp.sum(t, axis=1, keepdims=True)
        weighed = jnp.sum(t * c, axis=1, keepdims=True)
        lines = rate[i]
        spread_lines = jnp.concatenate([jnp.broadcast_to(lines[h:h + 1, :], (long, long)) for h in range(high)], axis=0)
        speed = jnp.sum(jnp.where(diagonal, spread_lines, 0.0), axis=1, keepdims=True)
        state[here, :] = c + speed * (lagged - totals * c - weighed)
        return carry

    lax.fori_loop(0, cells // tile, react, 0)

    def scatter(i, carry):
        for j in range(step):
            a = i * step + j
            row = state[pl.ds(a, 1), :]
            at = [pl.ds(index[k][a], 1) for k in range(corners)]
            new = [accs[k][at[k], :] + row * wide[pl.ds(a * corners + k, 1), :] for k in range(corners)]
            for k in range(corners):
                accs[k][at[k], :] = new[k]
        return carry

    lax.fori_loop(0, cells // step, scatter, 0)
    chunk = 512

    def merge(i, carry):
        here = pl.ds(pl.multiple_of(i * chunk, chunk), chunk)
        total = accs[0][here, :]
        for acc in accs[1:]:
            total = total + acc[here, :]
        table[here, :] = total
        pltpu.make_async_copy(table.at[here], sums.at[here], out_sem).start()
        return carry

    lax.fori_loop(0, entries // chunk, merge, 0)
    pltpu.make_async_copy(table, sums, out_sem).wait()


def return_kernel(n_lat, n_lon, cells, cap, slots_in, sums, result, slots, out, back, slots_sem, own_sem, out_sem, send_sem,
                  recv_sem):
    place = Place(n_lat, n_lon)
    load = pltpu.make_async_copy(slots_in, slots, slots_sem)
    load.start()
    place.greet()

    def copy(u, v):
        b = 3 * u + v
        return pltpu.make_async_remote_copy(
            src_ref=sums.at[pl.ds(cells + slot(u, v) * cap, cap)], dst_ref=back.at[b], send_sem=send_sem.at[b],
            recv_sem=recv_sem.at[b], device_id=place.at(u, v), device_id_type=MESH)

    def send(pairs):
        for u, v in pairs:
            @pl.when(place.has(u))
            def _():
                copy(u, v).start()

    def sent(pairs):
        for u, v in pairs:
            @pl.when(place.has(u))
            def _():
                copy(u, v).wait_send()

    tile = 256
    bins = out.shape[1]
    number = lax.broadcasted_iota(I32, (tile, bins), 0).astype(I16)

    def collect(pairs):
        for u, v in pairs:
            @pl.when(place.has(2 - u))
            def _():
                b = 3 * u + v
                copy(u, v).wait_recv()
                rows = jnp.concatenate(split(back[b]), axis=1)
                lines = cap // bins
                named = [slots[pl.ds(b * lines + q, 1), :] for q in range(lines)]

                def add(i, carry):
                    here = pl.ds(pl.multiple_of(i * tile, tile), tile)
                    hits = [(line - i * tile).astype(I16) == number for line in named]
                    pick = jnp.concatenate(
                        [jnp.where(hit, jnp.ones((), BF16), jnp.zeros((), BF16)) for hit in hits], axis=1)
                    got = jnp.dot(pick, rows, preferred_element_type=F32)
                    out[here, :] += got[:, :bins] + got[:, bins:]
                    if (u, v) == BACK[5]:
                        pltpu.make_async_copy(out.at[here], result.at[here], out_sem).start()
                    return carry

                lax.fori_loop(0, cells // tile, add, 0)

    send(BACK[:4])
    send(BACK[6:])
    keep = pltpu.make_async_copy(sums.at[pl.ds(0, cells)], out, own_sem)
    keep.start()
    load.wait()
    keep.wait()
    collect(BACK[6:])
    sent(BACK[:2])
    send(BACK[4:6])
    collect(BACK[:6])
    sent(BACK[2:])
    pltpu.make_async_copy(out, result, out_sem).wait()


def copy_kernel(source, target, held, in_sem, out_sem):
    part = source.shape[0] // 4
    parts = [pl.ds(n * part, part) for n in range(4)]
    loads = [pltpu.make_async_copy(source.at[here], held.at[here], in_sem.at[n]) for n, here in enumerate(parts)]
    stores = [pltpu.make_async_copy(held.at[here], target.at[here], out_sem.at[n]) for n, here in enumerate(parts)]
    for load in loads:
        load.start()
    for load, store in zip(loads, stores):
        load.wait()
        store.start()
    for store in stores:
        store.wait()


def on_device(n_lat, n_lon, concentration, cotangent, coag_rate, weights, departure, send_list):
    levels, lat_cells, lon_cells, bins = concentration.shape
    cells = levels * lat_cells * lon_cells
    blocks, cap = send_list.shape[2:]
    corners = departure.shape[0]
    entries = cells + (blocks - 1) * cap
    own = concentration.reshape(cells, bins)
    dma = pltpu.SemaphoreType.DMA
    table, spread, named = pl.pallas_call(
        functools.partial(send_kernel, n_lat, n_lon, cells, cap),
        out_shape=[jax.ShapeDtypeStruct((entries, bins), F32), jax.ShapeDtypeStruct((cells * corners, bins), F32),
                   jax.ShapeDtypeStruct((corners * cells // bins, bins), I32)],
        in_specs=[ANY] * 4, out_specs=[ANY, ANY, ANY],
        scratch_shapes=[pltpu.SMEM((blocks * cap,), I32), pltpu.VMEM((cells, bins), F32),
                        pltpu.VMEM(weights.shape, F32), pltpu.VMEM(departure.shape, I32),
                        pltpu.VMEM((blocks, cap, bins), F32), pltpu.VMEM((cells * corners, bins), F32),
                        pltpu.VMEM((corners * cells // bins, bins), I32), dma((4,)), dma, dma, dma, dma((blocks,)), dma((blocks,)),
                        dma((4,)), dma((4,))],
        compiler_params=pltpu.CompilerParams(
            collective_id=0, has_side_effects=True, vmem_limit_bytes=60 * 2**20),
    )(send_list.reshape(blocks * cap), own, weights, departure)
    forward, inverse = spectral_tables(bins)
    fwd_hi, fwd_lo = split(jnp.asarray(forward))
    inv_hi, inv_lo = split(jnp.asarray(inverse))
    sums = pl.pallas_call(
        functools.partial(cell_kernel, cells, corners),
        out_shape=jax.ShapeDtypeStruct((entries, bins), F32),
        in_specs=[ANY] * 9, out_specs=ANY,
        scratch_shapes=[pltpu.VMEM((entries, bins), F32), pltpu.VMEM((cells, bins), F32),
                        pltpu.VMEM((cells * corners, bins), F32), pltpu.VMEM((cells, bins), F32),
                        pltpu.VMEM(coag_rate.shape, F32)]
        + [pltpu.VMEM(part.shape, BF16) for part in (fwd_hi, fwd_lo, inv_hi, inv_lo)]
        + [pltpu.VMEM((entries, bins), F32)] * corners + [pltpu.SMEM((cells,), I32)] * corners
        + [dma((corners,)), dma, dma((PARTS,)), dma((6,)), dma],
        compiler_params=pltpu.CompilerParams(vmem_limit_bytes=60 * 2**20),
    )(named.reshape(-1), spread, table, cotangent.reshape(cells, bins), coag_rate, fwd_hi, fwd_lo,
      inv_hi, inv_lo)
    total = pl.pallas_call(
        functools.partial(return_kernel, n_lat, n_lon, cells, cap),
        out_shape=jax.ShapeDtypeStruct((cells, bins), F32),
        in_specs=[ANY, ANY], out_specs=ANY,
        scratch_shapes=[pltpu.VMEM((blocks * cap // bins, bins), I32), pltpu.VMEM((cells, bins), F32),
                        pltpu.VMEM((blocks, cap, bins), F32), dma, dma, dma,
                        dma((blocks,)), dma((blocks,))],
        compiler_params=pltpu.CompilerParams(
            collective_id=1, has_side_effects=True, vmem_limit_bytes=60 * 2**20),
    )(send_list.reshape(blocks * cap // bins, bins), sums)
    total = pl.pallas_call(
        copy_kernel, out_shape=jax.ShapeDtypeStruct((cells, bins), F32), in_specs=[ANY], out_specs=ANY,
        scratch_shapes=[pltpu.VMEM((cells, bins), F32), dma((4,)), dma((4,))],
        compiler_params=pltpu.CompilerParams(vmem_limit_bytes=60 * 2**20))(total)
    return total.reshape(levels, lat_cells, lon_cells, bins)


def solution(mesh):
    grid = P(None, "lat", "lon", None)
    field = P(None, "lat", "lon")
    corner = P(None, None, "lat", "lon")
    lists = P("lat", "lon", None, None)
    body = functools.partial(on_device, mesh.shape["lat"], mesh.shape["lon"])
    return jax.shard_map(
        body, mesh=mesh, in_specs=(grid, grid, field, corner, corner, lists), out_specs=grid, check_vma=False)
```

```python
import functools

import jax
import jax.numpy as jnp
import numpy as np
from jax import lax
from jax.experimental import pallas as pl
from jax.experimental.pallas import tpu as pltpu
from jax.sharding import PartitionSpec as P

MESH = pl.DeviceIdType.MESH
F32 = jnp.float32
BF16 = jnp.bfloat16
I16 = jnp.int16
I32 = jnp.int32
SMEM = pl.BlockSpec(memory_space=pltpu.SMEM)
VMEM = pl.BlockSpec(memory_space=pltpu.VMEM)
ANY = pl.BlockSpec(memory_space=pl.ANY)
FIRST = ((1, 0), (1, 2))
CORNER = ((0, 0), (2, 2), (0, 2), (2, 0))
REST = ((0, 1), (2, 1))
NEXT = CORNER + REST
BACK = CORNER + FIRST + REST

PARTS = 8


def split(x):
    hi = x.astype(BF16)
    return hi, (x - hi.astype(F32)).astype(BF16)


def spectral_tables(bins):
    period = 2 * bins
    k = np.arange(bins)
    n = np.arange(bins)[:, None]
    angle = 2.0 * np.pi * (n * k % period) / period
    sine = -np.sin(angle)
    sine[:, 0] = np.cos(np.pi * np.arange(bins))
    forward = np.concatenate([np.cos(angle), sine], axis=1)
    lag = np.arange(1, bins + 1)[None, :]
    back = 2.0 * np.pi * (k[:, None] * lag % period) / period
    scale = np.where(k == 0, 1.0, 2.0)[:, None] / period
    real = np.cos(back) * scale
    imag = -np.sin(back) * scale
    imag[0] = np.cos(np.pi * lag[0]) / period
    inverse = np.concatenate([real, imag], axis=0)
    return forward.astype(np.float32), inverse.astype(np.float32)


def slot(u, v):
    b = 3 * u + v
    return b - (b > 4)


class Place:
    def __init__(self, n_lat, n_lon):
        self.lat = lax.axis_index("lat")
        self.lon = lax.axis_index("lon")
        self.n_lat = n_lat
        self.n_lon = n_lon

    def has(self, u):
        there = self.lat + u - 1
        return (there >= 0) & (there < self.n_lat)

    def at(self, u, v):
        return (self.lat + u - 1, lax.rem(self.lon + v - 1 + self.n_lon, self.n_lon))

    def greet(self):
        barrier = pltpu.get_barrier_semaphore()
        for u, v in FIRST + NEXT:
            @pl.when(self.has(u))
            def _():
                pl.semaphore_signal(barrier, inc=1, device_id=self.at(u, v), device_id_type=MESH)
        count = jnp.where(self.lat > 0, 3, 0) + jnp.where(self.lat < self.n_lat - 1, 3, 0) + 2
        pl.semaphore_wait(barrier, count)


def send_kernel(n_lat, n_lon, cells, cap, slots_in, own_in, weights_in, departure_in, table, spread, named, slots, own,
                weights, departure, rows, wide, flat, in_sem, own_sem, wide_sem, flat_sem, send_sem, recv_sem, half_send,
                half_recv):
    pairs = ((slots_in, slots), (own_in, own), (weights_in, weights), (departure_in, departure))
    loads = [pltpu.make_async_copy(source, target, in_sem.at[n]) for n, (source, target) in enumerate(pairs)]
    for load in loads:
        load.start()
    place = Place(n_lat, n_lon)
    place.greet()
    keep = pltpu.make_async_copy(own, table.at[pl.ds(0, cells)], own_sem)
    loads[0].wait()
    loads[1].wait()

    def copy(u, v):
        b = 3 * u + v
        return pltpu.make_async_remote_copy(
            src_ref=rows.at[b], dst_ref=table.at[pl.ds(cells + slot(u, v) * cap, cap)], send_sem=send_sem.at[b],
            recv_sem=recv_sem.at[b], device_id=place.at(2 - u, 2 - v), device_id_type=MESH)

    half = cap // 2

    def half_copy(u, v, h):
        b = 3 * u + v
        sem = 2 * (v // 2) + h
        return pltpu.make_async_remote_copy(
            src_ref=rows.at[b, pl.ds(h * half, half)],
            dst_ref=table.at[pl.ds(cells + slot(u, v) * cap + h * half, half)], send_sem=half_send.at[sem],
            recv_sem=half_recv.at[sem], device_id=place.at(2 - u, 2 - v), device_id_type=MESH)

    def pick(b, low, count):
        step = 32

        def gather(i, carry):
            for j in range(step):
                s = low + i * step + j
                rows[b, pl.ds(s, 1), :] = own[pl.ds(slots[b * cap + s], 1), :]
            return carry

        lax.fori_loop(0, count // step, gather, 0)

    for h in range(2):
        for u, v in FIRST:
            pick(3 * u + v, h * half, half)
            half_copy(u, v, h).start()
    for u, v in NEXT:
        @pl.when(place.has(2 - u))
        def _():
            pick(3 * u + v, 0, cap)
            copy(u, v).start()
    keep.start()
    loads[2].wait()
    loads[3].wait()
    corners, levels, high, long = weights.shape
    bins = own.shape[1]
    per_level = high * long * corners

    def widen(level, carry):
        values = weights[:, level]
        start = level * per_level
        for i in range(high):
            line = values[:, i, :]
            for j in range(long):
                at = pl.multiple_of(start + (i * long + j) * corners, corners)
                wide[pl.ds(at, corners), :] = jnp.broadcast_to(line[:, j:j + 1], (corners, bins))
        return carry

    lax.fori_loop(0, levels, widen, 0)
    store = pltpu.make_async_copy(wide, spread, wide_sem)
    store.start()
    packs = bins // long
    mine = lax.broadcasted_iota(I32, (high, bins), 1) // long == lax.broadcasted_iota(I32, (high, bins), 0) % packs

    def flatten(k, carry):
        lines = []
        for level in range(levels):
            value = departure[k, level]
            value = jnp.where(value < cells + 5 * cap, value, value - cap)
            value = jnp.where(mine, jnp.concatenate([value] * packs, axis=1), 0)
            lines += [jnp.sum(value[h:h + packs], axis=0, keepdims=True) for h in range(0, high, packs)]
        count = len(lines)
        flat[pl.ds(pl.multiple_of(k * count, count), count), :] = jnp.concatenate(lines, axis=0)
        return carry

    lax.fori_loop(0, corners, flatten, 0)
    note = pltpu.make_async_copy(flat, named, flat_sem)
    note.start()
    keep.wait()
    store.wait()
    note.wait()
    for h in range(2):
        for u, v in FIRST:
            half_copy(u, v, h).wait_recv()
            half_copy(u, v, h).wait_send()
    for u, v in NEXT:
        @pl.when(place.has(u))
        def _():
            copy(u, v).wait_recv()

        @pl.when(place.has(2 - u))
        def _():
            copy(u, v).wait_send()


def cell_kernel(cells, corners, *refs):
    (named, spread, table_hbm), later_in, sums, refs = refs[:3], refs[3:9], refs[9], refs[10:]
    (table, state, wide), later, refs = refs[:3], refs[3:9], refs[9:]
    cot, rate, fwd_hi, fwd_lo, inv_hi, inv_lo = later
    accs, refs = refs[:corners], refs[corners:]
    index, (index_sem, table_sem, wide_sem, later_sem, out_sem) = refs[:corners], refs[corners:]
    entries, bins = table.shape
    load = pltpu.make_async_copy(table_hbm, table, table_sem)
    load.start()
    loads = [pltpu.make_async_copy(named.at[pl.ds(k * cells, cells)], index[k], index_sem.at[k]) for k in range(corners)]
    for copy in loads:
        copy.start()
    part = cells // PARTS

    def wide_copy(p):
        here = pl.ds(pl.multiple_of(p * part * corners, part * corners), part * corners)
        return pltpu.make_async_copy(spread.at[here], wide.at[here], wide_sem.at[p])

    for p in range(2):
        wide_copy(p).start()
    for copy in loads:
        copy.wait()
    load.wait()
    for p in range(2, PARTS):
        wide_copy(p).start()
    laters = [pltpu.make_async_copy(source, target, later_sem.at[n])
              for n, (source, target) in enumerate(zip(later_in, later))]
    for copy in laters:
        copy.start()
    near = 16
    clear = entries * near // cells

    def gather(i, carry):
        for j in range(near):
            a = i * near + j
            total = None
            for k in range(corners):
                row = table[pl.ds(index[k][a], 1), :] * wide[pl.ds(a * corners + k, 1), :]
                total = row if total is None else total + row
            state[pl.ds(a, 1), :] = total
        for acc in accs:
            acc[pl.ds(pl.multiple_of(i * clear, clear), clear), :] = jnp.zeros((clear, bins), F32)
        return carry

    def next_part(p, carry):
        wide_copy(p).wait()
        lax.fori_loop(p * (part // near), (p + 1) * (part // near), gather, 0)
        return carry

    lax.fori_loop(0, PARTS, next_part, 0)
    for copy in laters:
        copy.wait()
    levels, high, long = rate.shape
    tile = high * long
    first = lax.broadcasted_iota(I32, (tile, bins), 1) == 0
    diagonal = lax.broadcasted_iota(I32, (tile, long), 0) % long == lax.broadcasted_iota(I32, (tile, long), 1)

    def dot3(x, hi, lo):
        xh, xl = split(x)
        out = jnp.dot(xh, hi[...], preferred_element_type=F32)
        out += jnp.dot(xl, hi[...], preferred_element_type=F32)
        return out + jnp.dot(xh, lo[...], preferred_element_type=F32)

    def react(i, carry):
        here = pl.ds(pl.multiple_of(i * tile, tile), tile)
        t = state[here, :]
        c = cot[here, :]
        ts = dot3(t, fwd_hi, fwd_lo)
        cs = dot3(c, fwd_hi, fwd_lo)
        ta, tb, ca, cb = ts[:, :bins], ts[:, bins:], cs[:, :bins], cs[:, bins:]
        both = tb * cb
        real = ta * ca + jnp.where(first, 0.0, both)
        imag = jnp.where(first, both, ta * cb - tb * ca)
        lagged = dot3(jnp.concatenate([real, imag], axis=1), inv_hi, inv_lo)
        totals = jnp.sum(t, axis=1, keepdims=True)
        weighed = jnp.sum(t * c, axis=1, keepdims=True)
        lines = rate[i]
        spread_lines = jnp.concatenate([jnp.broadcast_to(lines[h:h + 1, :], (long, long)) for h in range(high)], axis=0)
        speed = jnp.sum(jnp.where(diagonal, spread_lines, 0.0), axis=1, keepdims=True)
        state[here, :] = c + speed * (lagged - totals * c - weighed)
        return carry

    lax.fori_loop(0, cells // tile, react, 0)

    step = 32
    def scatter(i, carry):
        for j in range(step):
            a = i * step + j
            row = state[pl.ds(a, 1), :]
            at = [pl.ds(index[k][a], 1) for k in range(corners)]
            new = [accs[k][at[k], :] + row * wide[pl.ds(a * corners + k, 1), :] for k in range(corners)]
            for k in range(corners):
                accs[k][at[k], :] = new[k]
        return carry

    lax.fori_loop(0, cells // step, scatter, 0)
    chunk = 512

    def merge(i, carry):
        here = pl.ds(pl.multiple_of(i * chunk, chunk), chunk)
        total = accs[0][here, :]
        for acc in accs[1:]:
            total = total + acc[here, :]
        table[here, :] = total
        pltpu.make_async_copy(table.at[here], sums.at[here], out_sem).start()
        return carry

    lax.fori_loop(0, entries // chunk, merge, 0)
    pltpu.make_async_copy(table, sums, out_sem).wait()


def return_kernel(n_lat, n_lon, cells, cap, slots_in, sums, result, slots, out, back, slots_sem, own_sem, out_sem, send_sem,
                  recv_sem):
    place = Place(n_lat, n_lon)
    load = pltpu.make_async_copy(slots_in, slots, slots_sem)
    load.start()
    place.greet()

    def copy(u, v):
        b = 3 * u + v
        return pltpu.make_async_remote_copy(
            src_ref=sums.at[pl.ds(cells + slot(u, v) * cap, cap)], dst_ref=back.at[b], send_sem=send_sem.at[b],
            recv_sem=recv_sem.at[b], device_id=place.at(u, v), device_id_type=MESH)

    def send(pairs):
        for u, v in pairs:
            @pl.when(place.has(u))
            def _():
                copy(u, v).start()

    def sent(pairs):
        for u, v in pairs:
            @pl.when(place.has(u))
            def _():
                copy(u, v).wait_send()

    tile = 256
    bins = out.shape[1]
    number = lax.broadcasted_iota(I32, (tile, bins), 0).astype(I16)

    def collect(pairs):
        for u, v in pairs:
            @pl.when(place.has(2 - u))
            def _():
                b = 3 * u + v
                copy(u, v).wait_recv()
                rows = jnp.concatenate(split(back[b]), axis=1)
                lines = cap // bins
                named = [slots[pl.ds(b * lines + q, 1), :] for q in range(lines)]

                def add(i, carry):
                    here = pl.ds(pl.multiple_of(i * tile, tile), tile)
                    hits = [(line - i * tile).astype(I16) == number for line in named]
                    pick = jnp.concatenate(
                        [jnp.where(hit, jnp.ones((), BF16), jnp.zeros((), BF16)) for hit in hits], axis=1)
                    got = jnp.dot(pick, rows, preferred_element_type=F32)
                    out[here, :] += got[:, :bins] + got[:, bins:]
                    if (u, v) == BACK[5]:
                        pltpu.make_async_copy(out.at[here], result.at[here], out_sem).start()
                    return carry

                lax.fori_loop(0, cells // tile, add, 0)

    send(BACK[:4])
    send(BACK[6:])
    keep = pltpu.make_async_copy(sums.at[pl.ds(0, cells)], out, own_sem)
    keep.start()
    load.wait()
    keep.wait()
    for n in range(2):
        collect(BACK[6 + n:7 + n])
    for n in range(2):
        sent(BACK[n:n + 1])
        send(BACK[4 + n:5 + n])
    collect(BACK[:6])
    sent(BACK[2:])
    pltpu.make_async_copy(out, result, out_sem).wait()


def copy_kernel(source, target, held, in_sem, out_sem):
    part = source.shape[0] // 4
    parts = [pl.ds(n * part, part) for n in range(4)]
    loads = [pltpu.make_async_copy(source.at[here], held.at[here], in_sem.at[n]) for n, here in enumerate(parts)]
    stores = [pltpu.make_async_copy(held.at[here], target.at[here], out_sem.at[n]) for n, here in enumerate(parts)]
    for load in loads:
        load.start()
    for load, store in zip(loads, stores):
        load.wait()
        store.start()
    for store in stores:
        store.wait()


def on_device(n_lat, n_lon, concentration, cotangent, coag_rate, weights, departure, send_list):
    levels, lat_cells, lon_cells, bins = concentration.shape
    cells = levels * lat_cells * lon_cells
    blocks, cap = send_list.shape[2:]
    corners = departure.shape[0]
    entries = cells + (blocks - 1) * cap
    own = concentration.reshape(cells, bins)
    dma = pltpu.SemaphoreType.DMA
    table, spread, named = pl.pallas_call(
        functools.partial(send_kernel, n_lat, n_lon, cells, cap),
        out_shape=[jax.ShapeDtypeStruct((entries, bins), F32), jax.ShapeDtypeStruct((cells * corners, bins), F32),
                   jax.ShapeDtypeStruct((corners * cells // bins, bins), I32)],
        in_specs=[ANY] * 4, out_specs=[ANY, ANY, ANY],
        scratch_shapes=[pltpu.SMEM((blocks * cap,), I32), pltpu.VMEM((cells, bins), F32),
                        pltpu.VMEM(weights.shape, F32), pltpu.VMEM(departure.shape, I32),
                        pltpu.VMEM((blocks, cap, bins), F32), pltpu.VMEM((cells * corners, bins), F32),
                        pltpu.VMEM((corners * cells // bins, bins), I32), dma((4,)), dma, dma, dma, dma((blocks,)), dma((blocks,)),
                        dma((4,)), dma((4,))],
        compiler_params=pltpu.CompilerParams(
            collective_id=0, has_side_effects=True, vmem_limit_bytes=60 * 2**20),
    )(send_list.reshape(blocks * cap), own, weights, departure)
    forward, inverse = spectral_tables(bins)
    fwd_hi, fwd_lo = split(jnp.asarray(forward))
    inv_hi, inv_lo = split(jnp.asarray(inverse))
    sums = pl.pallas_call(
        functools.partial(cell_kernel, cells, corners),
        out_shape=jax.ShapeDtypeStruct((entries, bins), F32),
        in_specs=[ANY] * 9, out_specs=ANY,
        scratch_shapes=[pltpu.VMEM((entries, bins), F32), pltpu.VMEM((cells, bins), F32),
                        pltpu.VMEM((cells * corners, bins), F32), pltpu.VMEM((cells, bins), F32),
                        pltpu.VMEM(coag_rate.shape, F32)]
        + [pltpu.VMEM(part.shape, BF16) for part in (fwd_hi, fwd_lo, inv_hi, inv_lo)]
        + [pltpu.VMEM((entries, bins), F32)] * corners + [pltpu.SMEM((cells,), I32)] * corners
        + [dma((corners,)), dma, dma((PARTS,)), dma((6,)), dma],
        compiler_params=pltpu.CompilerParams(vmem_limit_bytes=60 * 2**20),
    )(named.reshape(-1), spread, table, cotangent.reshape(cells, bins), coag_rate, fwd_hi, fwd_lo,
      inv_hi, inv_lo)
    total = pl.pallas_call(
        functools.partial(return_kernel, n_lat, n_lon, cells, cap),
        out_shape=jax.ShapeDtypeStruct((cells, bins), F32),
        in_specs=[ANY, ANY], out_specs=ANY,
        scratch_shapes=[pltpu.VMEM((blocks * cap // bins, bins), I32), pltpu.VMEM((cells, bins), F32),
                        pltpu.VMEM((blocks, cap, bins), F32), dma, dma, dma,
                        dma((blocks,)), dma((blocks,))],
        compiler_params=pltpu.CompilerParams(
            collective_id=1, has_side_effects=True, vmem_limit_bytes=60 * 2**20),
    )(send_list.reshape(blocks * cap // bins, bins), sums)
    total = pl.pallas_call(
        copy_kernel, out_shape=jax.ShapeDtypeStruct((cells, bins), F32), in_specs=[ANY], out_specs=ANY,
        scratch_shapes=[pltpu.VMEM((cells, bins), F32), dma((4,)), dma((4,))],
        compiler_params=pltpu.CompilerParams(vmem_limit_bytes=60 * 2**20))(total)
    return total.reshape(levels, lat_cells, lon_cells, bins)


def solution(mesh):
    grid = P(None, "lat", "lon", None)
    field = P(None, "lat", "lon")
    corner = P(None, None, "lat", "lon")
    lists = P("lat", "lon", None, None)
    body = functools.partial(on_device, mesh.shape["lat"], mesh.shape["lon"])
    return jax.shard_map(
        body, mesh=mesh, in_specs=(grid, grid, field, corner, corner, lists), out_specs=grid, check_vma=False)
```

```python
import functools

import jax
import jax.numpy as jnp
import numpy as np
from jax import lax
from jax.experimental import pallas as pl
from jax.experimental.pallas import tpu as pltpu
from jax.sharding import PartitionSpec as P

MESH = pl.DeviceIdType.MESH
F32 = jnp.float32
BF16 = jnp.bfloat16
I16 = jnp.int16
I32 = jnp.int32
SMEM = pl.BlockSpec(memory_space=pltpu.SMEM)
VMEM = pl.BlockSpec(memory_space=pltpu.VMEM)
ANY = pl.BlockSpec(memory_space=pl.ANY)
FIRST = ((1, 0), (1, 2))
CORNER = ((0, 0), (2, 2), (0, 2), (2, 0))
REST = ((0, 1), (2, 1))
NEXT = CORNER + REST
BACK = CORNER + FIRST + REST

PARTS = 8


def split(x):
    hi = x.astype(BF16)
    return hi, (x - hi.astype(F32)).astype(BF16)


def spectral_tables(bins):
    period = 2 * bins
    k = np.arange(bins)
    n = np.arange(bins)[:, None]
    angle = 2.0 * np.pi * (n * k % period) / period
    sine = -np.sin(angle)
    sine[:, 0] = np.cos(np.pi * np.arange(bins))
    forward = np.concatenate([np.cos(angle), sine], axis=1)
    lag = np.arange(1, bins + 1)[None, :]
    back = 2.0 * np.pi * (k[:, None] * lag % period) / period
    scale = np.where(k == 0, 1.0, 2.0)[:, None] / period
    real = np.cos(back) * scale
    imag = -np.sin(back) * scale
    imag[0] = np.cos(np.pi * lag[0]) / period
    inverse = np.concatenate([real, imag], axis=0)
    return forward.astype(np.float32), inverse.astype(np.float32)


def slot(u, v):
    b = 3 * u + v
    return b - (b > 4)


class Place:
    def __init__(self, n_lat, n_lon):
        self.lat = lax.axis_index("lat")
        self.lon = lax.axis_index("lon")
        self.n_lat = n_lat
        self.n_lon = n_lon

    def has(self, u):
        there = self.lat + u - 1
        return (there >= 0) & (there < self.n_lat)

    def at(self, u, v):
        return (self.lat + u - 1, lax.rem(self.lon + v - 1 + self.n_lon, self.n_lon))

    def greet(self):
        barrier = pltpu.get_barrier_semaphore()
        for u, v in FIRST + NEXT:
            @pl.when(self.has(u))
            def _():
                pl.semaphore_signal(barrier, inc=1, device_id=self.at(u, v), device_id_type=MESH)
        count = jnp.where(self.lat > 0, 3, 0) + jnp.where(self.lat < self.n_lat - 1, 3, 0) + 2
        pl.semaphore_wait(barrier, count)


def send_kernel(n_lat, n_lon, cells, cap, slots_in, own_in, weights_in, departure_in, table, spread, named, slots, own,
                weights, departure, rows, wide, flat, in_sem, own_sem, wide_sem, flat_sem, send_sem, recv_sem, piece_send,
                piece_recv):
    pairs = ((slots_in, slots), (own_in, own), (weights_in, weights), (departure_in, departure))
    loads = [pltpu.make_async_copy(source, target, in_sem.at[n]) for n, (source, target) in enumerate(pairs)]
    for load in loads:
        load.start()
    place = Place(n_lat, n_lon)
    place.greet()
    keep = pltpu.make_async_copy(own, table.at[pl.ds(0, cells)], own_sem)
    loads[0].wait()
    loads[1].wait()

    def copy(u, v):
        b = 3 * u + v
        return pltpu.make_async_remote_copy(
            src_ref=rows.at[b], dst_ref=table.at[pl.ds(cells + slot(u, v) * cap, cap)], send_sem=send_sem.at[b],
            recv_sem=recv_sem.at[b], device_id=place.at(2 - u, 2 - v), device_id_type=MESH)

    pieces = 4
    size = cap // pieces

    def piece_copy(u, v, h):
        b = 3 * u + v
        sem = pieces * (v // 2) + h
        return pltpu.make_async_remote_copy(
            src_ref=rows.at[b, pl.ds(h * size, size)],
            dst_ref=table.at[pl.ds(cells + slot(u, v) * cap + h * size, size)], send_sem=piece_send.at[sem],
            recv_sem=piece_recv.at[sem], device_id=place.at(2 - u, 2 - v), device_id_type=MESH)

    def pick(b, low, count):
        step = 32

        def gather(i, carry):
            for j in range(step):
                s = low + i * step + j
                rows[b, pl.ds(s, 1), :] = own[pl.ds(slots[b * cap + s], 1), :]
            return carry

        lax.fori_loop(0, count // step, gather, 0)

    for h in range(pieces):
        for u, v in FIRST:
            pick(3 * u + v, h * size, size)
            piece_copy(u, v, h).start()
    for u, v in NEXT:
        @pl.when(place.has(2 - u))
        def _():
            pick(3 * u + v, 0, cap)
            copy(u, v).start()
    keep.start()
    loads[2].wait()
    loads[3].wait()
    corners, levels, high, long = weights.shape
    bins = own.shape[1]
    per_level = high * long * corners

    def widen(level, carry):
        values = weights[:, level]
        start = level * per_level
        for i in range(high):
            line = values[:, i, :]
            for j in range(long):
                at = pl.multiple_of(start + (i * long + j) * corners, corners)
                wide[pl.ds(at, corners), :] = jnp.broadcast_to(line[:, j:j + 1], (corners, bins))
        return carry

    lax.fori_loop(0, levels, widen, 0)
    store = pltpu.make_async_copy(wide, spread, wide_sem)
    store.start()
    packs = bins // long
    mine = lax.broadcasted_iota(I32, (high, bins), 1) // long == lax.broadcasted_iota(I32, (high, bins), 0) % packs

    def flatten(k, carry):
        lines = []
        for level in range(levels):
            value = departure[k, level]
            value = jnp.where(value < cells + 5 * cap, value, value - cap)
            value = jnp.where(mine, jnp.concatenate([value] * packs, axis=1), 0)
            lines += [jnp.sum(value[h:h + packs], axis=0, keepdims=True) for h in range(0, high, packs)]
        count = len(lines)
        flat[pl.ds(pl.multiple_of(k * count, count), count), :] = jnp.concatenate(lines, axis=0)
        return carry

    lax.fori_loop(0, corners, flatten, 0)
    note = pltpu.make_async_copy(flat, named, flat_sem)
    note.start()
    keep.wait()
    store.wait()
    note.wait()
    for h in range(pieces):
        for u, v in FIRST:
            piece_copy(u, v, h).wait_recv()
            piece_copy(u, v, h).wait_send()
    for u, v in NEXT:
        @pl.when(place.has(u))
        def _():
            copy(u, v).wait_recv()

        @pl.when(place.has(2 - u))
        def _():
            copy(u, v).wait_send()


def cell_kernel(cells, corners, *refs):
    (named, spread, table_hbm), later_in, sums, refs = refs[:3], refs[3:9], refs[9], refs[10:]
    (table, state, wide), later, refs = refs[:3], refs[3:9], refs[9:]
    cot, rate, fwd_hi, fwd_lo, inv_hi, inv_lo = later
    accs, refs = refs[:corners], refs[corners:]
    index, (index_sem, table_sem, wide_sem, later_sem, out_sem) = refs[:corners], refs[corners:]
    entries, bins = table.shape
    load = pltpu.make_async_copy(table_hbm, table, table_sem)
    load.start()
    loads = [pltpu.make_async_copy(named.at[pl.ds(k * cells, cells)], index[k], index_sem.at[k]) for k in range(corners)]
    for copy in loads:
        copy.start()
    part = cells // PARTS

    def wide_copy(p):
        here = pl.ds(pl.multiple_of(p * part * corners, part * corners), part * corners)
        return pltpu.make_async_copy(spread.at[here], wide.at[here], wide_sem.at[p])

    for p in range(2):
        wide_copy(p).start()
    for copy in loads:
        copy.wait()
    load.wait()
    for p in range(2, PARTS):
        wide_copy(p).start()
    laters = [pltpu.make_async_copy(source, target, later_sem.at[n])
              for n, (source, target) in enumerate(zip(later_in, later))]
    for copy in laters:
        copy.start()
    near = 16
    clear = entries * near // cells

    def gather(i, carry):
        for j in range(near):
            a = i * near + j
            total = None
            for k in range(corners):
                row = table[pl.ds(index[k][a], 1), :] * wide[pl.ds(a * corners + k, 1), :]
                total = row if total is None else total + row
            state[pl.ds(a, 1), :] = total
        for acc in accs:
            acc[pl.ds(pl.multiple_of(i * clear, clear), clear), :] = jnp.zeros((clear, bins), F32)
        return carry

    def next_part(p, carry):
        wide_copy(p).wait()
        lax.fori_loop(p * (part // near), (p + 1) * (part // near), gather, 0)
        return carry

    lax.fori_loop(0, PARTS, next_part, 0)
    for copy in laters:
        copy.wait()
    levels, high, long = rate.shape
    tile = high * long
    first = lax.broadcasted_iota(I32, (tile, bins), 1) == 0
    diagonal = lax.broadcasted_iota(I32, (tile, long), 0) % long == lax.broadcasted_iota(I32, (tile, long), 1)

    def dot3(x, hi, lo):
        xh, xl = split(x)
        out = jnp.dot(xh, hi[...], preferred_element_type=F32)
        out += jnp.dot(xl, hi[...], preferred_element_type=F32)
        return out + jnp.dot(xh, lo[...], preferred_element_type=F32)

    def react(i, carry):
        here = pl.ds(pl.multiple_of(i * tile, tile), tile)
        t = state[here, :]
        c = cot[here, :]
        ts = dot3(t, fwd_hi, fwd_lo)
        cs = dot3(c, fwd_hi, fwd_lo)
        ta, tb, ca, cb = ts[:, :bins], ts[:, bins:], cs[:, :bins], cs[:, bins:]
        both = tb * cb
        real = ta * ca + jnp.where(first, 0.0, both)
        imag = jnp.where(first, both, ta * cb - tb * ca)
        lagged = dot3(jnp.concatenate([real, imag], axis=1), inv_hi, inv_lo)
        totals = jnp.sum(t, axis=1, keepdims=True)
        weighed = jnp.sum(t * c, axis=1, keepdims=True)
        lines = rate[i]
        spread_lines = jnp.concatenate([jnp.broadcast_to(lines[h:h + 1, :], (long, long)) for h in range(high)], axis=0)
        speed = jnp.sum(jnp.where(diagonal, spread_lines, 0.0), axis=1, keepdims=True)
        state[here, :] = c + speed * (lagged - totals * c - weighed)
        return carry

    lax.fori_loop(0, cells // tile, react, 0)

    step = 32
    def scatter(i, carry):
        for j in range(step):
            a = i * step + j
            row = state[pl.ds(a, 1), :]
            at = [pl.ds(index[k][a], 1) for k in range(corners)]
            new = [accs[k][at[k], :] + row * wide[pl.ds(a * corners + k, 1), :] for k in range(corners)]
            for k in range(corners):
                accs[k][at[k], :] = new[k]
        return carry

    lax.fori_loop(0, cells // step, scatter, 0)
    chunk = 512

    def merge(i, carry):
        here = pl.ds(pl.multiple_of(i * chunk, chunk), chunk)
        total = accs[0][here, :]
        for acc in accs[1:]:
            total = total + acc[here, :]
        table[here, :] = total
        pltpu.make_async_copy(table.at[here], sums.at[here], out_sem).start()
        return carry

    lax.fori_loop(0, entries // chunk, merge, 0)
    pltpu.make_async_copy(table, sums, out_sem).wait()


def return_kernel(n_lat, n_lon, cells, cap, slots_in, sums, result, slots, out, back, slots_sem, own_sem, out_sem, send_sem,
                  recv_sem):
    place = Place(n_lat, n_lon)
    load = pltpu.make_async_copy(slots_in, slots, slots_sem)
    load.start()
    place.greet()

    def copy(u, v):
        b = 3 * u + v
        return pltpu.make_async_remote_copy(
            src_ref=sums.at[pl.ds(cells + slot(u, v) * cap, cap)], dst_ref=back.at[b], send_sem=send_sem.at[b],
            recv_sem=recv_sem.at[b], device_id=place.at(u, v), device_id_type=MESH)

    def send(pairs):
        for u, v in pairs:
            @pl.when(place.has(u))
            def _():
                copy(u, v).start()

    def sent(pairs):
        for u, v in pairs:
            @pl.when(place.has(u))
            def _():
                copy(u, v).wait_send()

    tile = 256
    bins = out.shape[1]
    number = lax.broadcasted_iota(I32, (tile, bins), 0).astype(I16)

    def collect(pairs):
        for u, v in pairs:
            @pl.when(place.has(2 - u))
            def _():
                b = 3 * u + v
                copy(u, v).wait_recv()
                rows = jnp.concatenate(split(back[b]), axis=1)
                lines = cap // bins
                named = [slots[pl.ds(b * lines + q, 1), :] for q in range(lines)]

                def add(i, carry):
                    here = pl.ds(pl.multiple_of(i * tile, tile), tile)
                    hits = [(line - i * tile).astype(I16) == number for line in named]
                    pick = jnp.concatenate(
                        [jnp.where(hit, jnp.ones((), BF16), jnp.zeros((), BF16)) for hit in hits], axis=1)
                    got = jnp.dot(pick, rows, preferred_element_type=F32)
                    out[here, :] += got[:, :bins] + got[:, bins:]
                    if (u, v) == BACK[5]:
                        pltpu.make_async_copy(out.at[here], result.at[here], out_sem).start()
                    return carry

                lax.fori_loop(0, cells // tile, add, 0)

    send(BACK[:4])
    send(BACK[6:])
    keep = pltpu.make_async_copy(sums.at[pl.ds(0, cells)], out, own_sem)
    keep.start()
    load.wait()
    keep.wait()
    for n in range(2):
        collect(BACK[6 + n:7 + n])
    for n in range(2):
        sent(BACK[n:n + 1])
        send(BACK[4 + n:5 + n])
    collect(BACK[:6])
    sent(BACK[2:])
    pltpu.make_async_copy(out, result, out_sem).wait()


def copy_kernel(source, target, held, in_sem, out_sem):
    part = source.shape[0] // 4
    parts = [pl.ds(n * part, part) for n in range(4)]
    loads = [pltpu.make_async_copy(source.at[here], held.at[here], in_sem.at[n]) for n, here in enumerate(parts)]
    stores = [pltpu.make_async_copy(held.at[here], target.at[here], out_sem.at[n]) for n, here in enumerate(parts)]
    for load in loads:
        load.start()
    for load, store in zip(loads, stores):
        load.wait()
        store.start()
    for store in stores:
        store.wait()


def on_device(n_lat, n_lon, concentration, cotangent, coag_rate, weights, departure, send_list):
    levels, lat_cells, lon_cells, bins = concentration.shape
    cells = levels * lat_cells * lon_cells
    blocks, cap = send_list.shape[2:]
    corners = departure.shape[0]
    entries = cells + (blocks - 1) * cap
    own = concentration.reshape(cells, bins)
    dma = pltpu.SemaphoreType.DMA
    table, spread, named = pl.pallas_call(
        functools.partial(send_kernel, n_lat, n_lon, cells, cap),
        out_shape=[jax.ShapeDtypeStruct((entries, bins), F32), jax.ShapeDtypeStruct((cells * corners, bins), F32),
                   jax.ShapeDtypeStruct((corners * cells // bins, bins), I32)],
        in_specs=[ANY] * 4, out_specs=[ANY, ANY, ANY],
        scratch_shapes=[pltpu.SMEM((blocks * cap,), I32), pltpu.VMEM((cells, bins), F32),
                        pltpu.VMEM(weights.shape, F32), pltpu.VMEM(departure.shape, I32),
                        pltpu.VMEM((blocks, cap, bins), F32), pltpu.VMEM((cells * corners, bins), F32),
                        pltpu.VMEM((corners * cells // bins, bins), I32), dma((4,)), dma, dma, dma, dma((blocks,)), dma((blocks,)),
                        dma((8,)), dma((8,))],
        compiler_params=pltpu.CompilerParams(
            collective_id=0, has_side_effects=True, vmem_limit_bytes=60 * 2**20),
    )(send_list.reshape(blocks * cap), own, weights, departure)
    forward, inverse = spectral_tables(bins)
    fwd_hi, fwd_lo = split(jnp.asarray(forward))
    inv_hi, inv_lo = split(jnp.asarray(inverse))
    sums = pl.pallas_call(
        functools.partial(cell_kernel, cells, corners),
        out_shape=jax.ShapeDtypeStruct((entries, bins), F32),
        in_specs=[ANY] * 9, out_specs=ANY,
        scratch_shapes=[pltpu.VMEM((entries, bins), F32), pltpu.VMEM((cells, bins), F32),
                        pltpu.VMEM((cells * corners, bins), F32), pltpu.VMEM((cells, bins), F32),
                        pltpu.VMEM(coag_rate.shape, F32)]
        + [pltpu.VMEM(part.shape, BF16) for part in (fwd_hi, fwd_lo, inv_hi, inv_lo)]
        + [pltpu.VMEM((entries, bins), F32)] * corners + [pltpu.SMEM((cells,), I32)] * corners
        + [dma((corners,)), dma, dma((PARTS,)), dma((6,)), dma],
        compiler_params=pltpu.CompilerParams(vmem_limit_bytes=60 * 2**20),
    )(named.reshape(-1), spread, table, cotangent.reshape(cells, bins), coag_rate, fwd_hi, fwd_lo,
      inv_hi, inv_lo)
    total = pl.pallas_call(
        functools.partial(return_kernel, n_lat, n_lon, cells, cap),
        out_shape=jax.ShapeDtypeStruct((cells, bins), F32),
        in_specs=[ANY, ANY], out_specs=ANY,
        scratch_shapes=[pltpu.VMEM((blocks * cap // bins, bins), I32), pltpu.VMEM((cells, bins), F32),
                        pltpu.VMEM((blocks, cap, bins), F32), dma, dma, dma,
                        dma((blocks,)), dma((blocks,))],
        compiler_params=pltpu.CompilerParams(
            collective_id=1, has_side_effects=True, vmem_limit_bytes=60 * 2**20),
    )(send_list.reshape(blocks * cap // bins, bins), sums)
    total = pl.pallas_call(
        copy_kernel, out_shape=jax.ShapeDtypeStruct((cells, bins), F32), in_specs=[ANY], out_specs=ANY,
        scratch_shapes=[pltpu.VMEM((cells, bins), F32), dma((4,)), dma((4,))],
        compiler_params=pltpu.CompilerParams(vmem_limit_bytes=60 * 2**20))(total)
    return total.reshape(levels, lat_cells, lon_cells, bins)


def solution(mesh):
    grid = P(None, "lat", "lon", None)
    field = P(None, "lat", "lon")
    corner = P(None, None, "lat", "lon")
    lists = P("lat", "lon", None, None)
    body = functools.partial(on_device, mesh.shape["lat"], mesh.shape["lon"])
    return jax.shard_map(
        body, mesh=mesh, in_specs=(grid, grid, field, corner, corner, lists), out_specs=grid, check_vma=False)
```
